256 devices in a mesh: cell: 16 (over y, z_lo), mem: 8 (over x, core), dp: 2 (over z_hi).
Axes of the slice: x: 4, y: 4, z: 8 (z_hi: 2, z_lo: 4; z = z_hi * 4 + z_lo), core: 2. Of those that a mesh axis runs over, the one named last changes fastest.
Arguments:
- ensemble: bfloat16 [256, 524288], P('mem', 'cell'), may hold values from -6 to 6
- data_anom: bfloat16 [256, 4096], P('mem', ('cell', 'dp')), may hold values from -6 to 6
- weighted_innov: bfloat16 [256, 4096], P('mem', ('cell', 'dp')), may hold values from -12 to 12
- profiles: bfloat16 [64, 128], replicated, may hold values from 0.049804688 to 1
- seg_data: int32 [128, 4096], P(('cell', 'dp')), may hold values from -1 to 4095, as said below
- seg_profile: int32 [128, 4096], P(('cell', 'dp')), may hold values from 0 to 63
Outputs:
- updated: bfloat16 [256, 524288], P('mem', ('cell', 'dp'))
The draws below stay inside these ranges and needn't reach their ends.
Inputs may be any that keep to these rules, and one draw needn't show every extreme that they name: `seg_data`: A slot holds -1 (empty) or a datum of its own data group: rows g * 4 to (g + 1) * 4 - 1 hold data 128 * g to 128 * (g + 1) - 1.
All inputs are finite; a program needn't handle non-finite values.
Results may differ from the reference program's by a relative error of at most 0.003.
Values may be sent and summed in bfloat16 or wider, within the bound.
No kernel may reach another device: no remote copies, remote signals or barrier semaphores. Data moves between devices by JAX's collectives and lax.ppermute only.
A program may use at most 128 MiB of HBM per device.

```python
import jax
import jax.numpy as jnp
from jax import lax

M = 256
ND = 4096
BLK = 128
NTAB = 64
KB = 4
BLOCKS = 4096
CELLS = 524288
DGROUPS = 32
DATA_GRP = 128


def draw_seg_data(key, part):
    first_key, second_key = jax.random.split(key)
    counts = jax.random.randint(first_key, (DGROUPS, 1, BLOCKS), 0, KB + 1)
    picks = jax.random.randint(second_key, (DGROUPS, KB, BLOCKS), 0, DATA_GRP)
    base_ids = jnp.arange(DGROUPS, dtype=jnp.int32)[:, None, None] * DATA_GRP
    slot_pos = jnp.arange(KB, dtype=jnp.int32)[None, :, None]
    chosen = jnp.where(slot_pos < counts, base_ids + picks, -1)
    chosen = chosen.at[DGROUPS - 1, 0, 0].set(ND - 1)
    chosen = chosen.at[0, KB - 1, 0].set(-1)
    return chosen.reshape(DGROUPS * KB, BLOCKS).astype(jnp.int32)


def touch_ends(values, rng, low, largest):
    longest = values.shape.index(max(values.shape))
    spots = []
    for shift in (0, 1):
        where = [jax.random.randint(jax.random.fold_in(rng, axis), (), 0, length) for axis, length in enumerate(values.shape)]
        where[longest] = (where[longest] + shift) % values.shape[longest]
        spots.append(tuple(where))
    return values.at[spots[0]].set(low).at[spots[1]].set(largest)


def level_of(rng, dims, cuts, least, high):
    level = 1.0
    for position, parts in cuts:
        steps = jax.random.uniform(jax.random.fold_in(jax.random.fold_in(rng, 6), position), (parts,), jnp.float32, least / len(cuts), high / len(cuts))
        level = level * jnp.repeat(jnp.exp(steps), dims[position] // parts).reshape((-1,) + (1,) * (len(dims) - 1 - position))
    return level


def normal_values(rng, shape, spread, reach, cuts=(), held_as=jnp.bfloat16):
    values = jax.random.normal(rng, shape, jnp.float32) * spread
    if len(cuts) > 0:
        values = level_of(rng, shape, cuts, -0.22, 0.18) * values
    return jnp.clip(values, min=-reach, max=reach).astype(held_as)


def setup_inputs(seed: int = 0) -> dict:
    streams_of = jax.random.split(jax.random.key(seed), 7)
    ensemble = normal_values(streams_of[0], (M, CELLS), 1.0, 6.0, ((0, 8), (1, 16)))
    data_anom = normal_values(streams_of[1], (M, ND), 1.0, 6.0, ((0, 8), (1, 32)))
    weighted_innov = normal_values(streams_of[2], (M, ND), 2.0, 12.0, ((0, 8), (1, 32)))
    profiles = jnp.clip(jax.random.uniform(streams_of[3], (NTAB, BLK), jnp.float32, 0.049804688, 1.0), 0.049804688, 1.0).astype(jnp.bfloat16)
    seg_data = draw_seg_data(jax.random.fold_in(streams_of[6], 71), 0)
    seg_profile = touch_ends(jax.random.randint(streams_of[5], (DGROUPS * KB, BLOCKS), 0, NTAB), jax.random.fold_in(streams_of[5], 1), 0, NTAB - 1).astype(jnp.int32)
    return dict(ensemble=ensemble, data_anom=data_anom, weighted_innov=weighted_innov, profiles=profiles, seg_data=seg_data, seg_profile=seg_profile)


def reference(ensemble, data_anom, weighted_innov, profiles, seg_data, seg_profile):
    state_blocks = ensemble.astype(jnp.float32).reshape(M, BLOCKS, BLK)
    anom_all = data_anom.astype(jnp.float32)
    innov_all = weighted_innov.astype(jnp.float32)
    table_rows = profiles.astype(jnp.float32)
    data_ids = seg_data.reshape(DGROUPS, KB, BLOCKS)
    prof_ids = seg_profile.reshape(DGROUPS, KB, BLOCKS)

    def one_group(running, inputs):
        group_ids, group_prof = inputs
        valid = group_ids >= 0
        safe_ids = jnp.where(valid, group_ids, 0).astype(jnp.int32)
        anom_cols = jnp.where(valid[None], anom_all[:, safe_ids], 0.0)
        innov_cols = jnp.where(valid[None], innov_all[:, safe_ids], 0.0)
        profile_rows = table_rows[group_prof]
        inner_prod = jnp.einsum("mbi,mkb->kbi", state_blocks, anom_cols, precision=lax.Precision.HIGHEST)
        rounded = (profile_rows * inner_prod / (M - 1)).astype(jnp.bfloat16)
        coefficient = lax.optimization_barrier(rounded).astype(jnp.float32)
        running = running + jnp.einsum("kbi,mkb->mbi", coefficient, innov_cols, precision=lax.Precision.HIGHEST)
        return running, None

    start_sum = jnp.zeros((M, BLOCKS, BLK), jnp.float32)
    correction, _ = lax.scan(one_group, start_sum, (data_ids, prof_ids))
    return (state_blocks.reshape(M, CELLS) + correction.reshape(M, CELLS)).astype(jnp.bfloat16)
```

```python
import jax
import jax.numpy as jnp
from jax import lax
from jax.experimental import pallas as pl
from jax.experimental.pallas import tpu as pltpu
from jax.sharding import PartitionSpec as P

M = 256
EMPTY = 512
X = 4
DN_NT = (((1,), (1,)), ((), ()))
DN_TN = (((0,), (0,)), ((), ()))


def update_kernel(*refs):
    data = (refs[0:4], refs[4:8])
    near_ref, far_ref, ids_ref, prof_ids_ref, table_ref, out_near, out_far, cols = refs[8:]
    n_group, two_m, data_dev = refs[0].shape
    mem_dev = two_m // 2
    half = X * mem_dev
    n_block = near_ref.shape[1] // 128
    n_slot = prof_ids_ref.shape[0]

    lanes = lax.broadcasted_iota(jnp.int32, (128, 2 * data_dev), 1).astype(jnp.float32)
    for pair in range(n_group // 2):
        picker = jnp.where(lanes == ids_ref[:, pair : pair + 1], 1.0, 0.0).astype(jnp.bfloat16)
        for side in range(2):
            values = jnp.concatenate(
                [
                    jnp.concatenate(
                        [data[side][s][2 * pair + g, a * mem_dev : (a + 1) * mem_dev, :] for a in range(2) for s in range(X)],
                        axis=0,
                    )
                    for g in range(2)
                ],
                axis=1,
            )
            picked = lax.dot_general(picker, values, DN_NT, preferred_element_type=jnp.float32)
            picked = picked.reshape(n_block, 8, 2 * half)
            for a in range(2):
                cols[a, :, pair * 8 : (pair + 1) * 8, side * half : (side + 1) * half] = picked[:, :, a * half : (a + 1) * half]

    table = table_ref[...]
    rows = lax.broadcasted_iota(jnp.int32, (n_slot, table.shape[0]), 1).astype(jnp.float32)
    for b in range(n_block):
        spot = pl.ds(b * 128, 128)
        state = jnp.concatenate([near_ref[:, spot], far_ref[:, spot]], axis=0)
        anom = cols[0, b].astype(jnp.bfloat16)
        innov = cols[1, b].astype(jnp.bfloat16)
        inner = jnp.dot(anom, state, preferred_element_type=jnp.float32)
        chooser = jnp.where(rows == prof_ids_ref[:, b : b + 1], 1.0, 0.0).astype(jnp.bfloat16)
        weight = jnp.dot(chooser, table, preferred_element_type=jnp.float32)
        coef = (weight * inner / (M - 1)).astype(jnp.bfloat16)
        corr = lax.dot_general(innov, coef, DN_TN, preferred_element_type=jnp.float32)
        new = (state.astype(jnp.float32) + corr).astype(jnp.bfloat16)
        out_near[:, spot] = new[:half]
        out_far[:, spot] = new[half:]


def run_update(data, near, far, ids, prof_ids, table):
    half, width = near.shape
    n_block = width // 128
    n_slot = prof_ids.shape[0]
    whole = pl.BlockSpec(memory_space=pltpu.VMEM)
    return pl.pallas_call(
        update_kernel,
        out_shape=[jax.ShapeDtypeStruct(near.shape, jnp.bfloat16)] * 2,
        in_specs=[whole] * 13,
        out_specs=[whole] * 2,
        scratch_shapes=[pltpu.VMEM((2, n_block, n_slot, 2 * half), jnp.float32)],
        compiler_params=pltpu.CompilerParams(vmem_limit_bytes=40 * 1024 * 1024),
        cost_estimate=pl.CostEstimate(flops=800_000_000, bytes_accessed=6_500_000, transcendentals=0),
        name="update",
    )(*data, near, far, ids, prof_ids, table)


def x_shift(s):
    return [(x * 2 + c, ((x + s) % X) * 2 + c) for x in range(X) for c in range(2)]


CORE_SWAP = [(i, i ^ 1) for i in range(2 * X)]
SHIFTS = (1, 3, 2)


def local(ensemble, data_anom, weighted_innov, profiles, seg_data, seg_profile):
    n_cell = lax.axis_size("cell")
    n_dp = lax.axis_size("dp")
    n_mem = lax.axis_size("mem")
    me_cell, me_dp, me_mem = (lax.axis_index(n) for n in ("cell", "dp", "mem"))
    me_x, me_core = me_mem // 2, me_mem % 2
    mem_dev, cells_dev = ensemble.shape
    data_dev = data_anom.shape[1]
    per_group, blocks = seg_data.shape
    n_group = n_cell * n_dp
    own_blocks = blocks // (n_group * n_mem)
    half_cells = cells_dev // n_dp
    x_cells = half_cells // X
    own_cells = x_cells // 2

    def mine(seg):
        seg = seg.reshape(per_group, n_group, n_mem * own_blocks)
        return lax.dynamic_slice_in_dim(seg, me_mem * own_blocks, own_blocks, 2)

    pair_ids = jnp.where(seg_data >= 0, seg_data - me_cell * (n_dp * data_dev), EMPTY)
    seg = jnp.concatenate([mine(pair_ids), mine(seg_profile)], axis=0).astype(jnp.bfloat16)
    seg = jnp.pad(seg.transpose(1, 0, 2), ((0, 0), (0, 0), (0, data_dev - own_blocks)))
    own_data = jnp.concatenate([data_anom, weighted_innov], axis=0)
    sent = jnp.concatenate([jnp.broadcast_to(own_data[None], (n_group,) + own_data.shape), seg], axis=1)

    got = lax.all_to_all(sent, ("cell", "dp"), 0, 0, tiled=True)

    def state_for(s):
        x_to = (me_x + s) % X
        return lax.dynamic_slice_in_dim(ensemble, me_dp * half_cells + x_to * x_cells, x_cells, 1)

    pieces = [state_for(0)] + [None] * 3
    for s in SHIFTS:
        pieces[s] = lax.ppermute(state_for(s), "mem", x_shift(s))
    state = jnp.concatenate(pieces, axis=0)
    near = lax.dynamic_slice_in_dim(state, me_core * own_cells, own_cells, 1)
    far = lax.ppermute(
        lax.dynamic_slice_in_dim(state, (1 - me_core) * own_cells, own_cells, 1), "mem", CORE_SWAP
    )

    data_near = [got[:, : 2 * mem_dev]] + [None] * 3
    for s in SHIFTS:
        data_near[s] = lax.ppermute(data_near[0], "mem", x_shift(s))
    data_far = [lax.ppermute(d, "mem", CORE_SWAP) for d in data_near]

    got_seg = got[:, 2 * mem_dev :, :own_blocks].astype(jnp.float32)
    ids = got_seg[:, :per_group].reshape(n_group // 2, 2 * per_group, own_blocks).transpose(2, 1, 0)
    ids = ids.reshape(own_blocks * 2 * per_group, n_group // 2)
    prof_ids = got_seg[:, per_group:].reshape(n_group * per_group, own_blocks)

    new_near, new_far = run_update(data_near + data_far, near, far, ids, prof_ids, profiles)

    back_far = lax.ppermute(new_far, "mem", CORE_SWAP)
    first = me_core == 0
    new = jnp.concatenate([jnp.where(first, new_near, back_far), jnp.where(first, back_far, new_near)], axis=1)
    out = jnp.zeros((mem_dev, half_cells), jnp.bfloat16)
    for s in (0,) + SHIFTS:
        piece = new[s * mem_dev : (s + 1) * mem_dev]
        if s:
            piece = lax.ppermute(piece, "mem", x_shift(X - s))
        out = lax.dynamic_update_slice_in_dim(out, piece, ((me_x + s) % X) * x_cells, 1)
    return out


def solution(mesh):
    placed = (
        P("mem", "cell"),
        P("mem", ("cell", "dp")),
        P("mem", ("cell", "dp")),
        P(),
        P(("cell", "dp"), None),
        P(("cell", "dp"), None),
    )
    return jax.shard_map(
        local, mesh=mesh, in_specs=placed, out_specs=P("mem", ("cell", "dp")), check_vma=False
    )
```

```python
import jax
import jax.numpy as jnp
from jax import lax
from jax.experimental import pallas as pl
from jax.experimental.pallas import tpu as pltpu
from jax.sharding import PartitionSpec as P

M = 256
EMPTY = 512
X, Y, Z = 4, 4, 8
DN_NT = (((1,), (1,)), ((), ()))
DN_TN = (((0,), (0,)), ((), ()))


def update_kernel(*refs):
    anom_data, innov_data = (refs[0:4], refs[4:8]), (refs[8:12], refs[12:16])
    near_ref, far_ref, ids_ref, prof_ids_ref, table_ref, out_near, out_far, cols = refs[16:]
    n_y, n_z, mem_dev, data_dev = refs[0].shape
    half = X * mem_dev
    n_block = near_ref.shape[1] // 128
    n_slot = prof_ids_ref.shape[0]

    lanes = lax.broadcasted_iota(jnp.int32, (128, 2 * data_dev), 1).astype(jnp.float32)
    for pair in range(n_y * n_z // 2):
        t, q = pair // (n_z // 2), pair % (n_z // 2)
        picker = jnp.where(lanes == ids_ref[:, pair : pair + 1], 1.0, 0.0).astype(jnp.bfloat16)
        for side in range(2):
            values = jnp.concatenate(
                [
                    jnp.concatenate(
                        [anom_data[side][s][t, 2 * q + g] for s in range(X)]
                        + [innov_data[side][t][s, 2 * q + g] for s in range(X)],
                        axis=0,
                    )
                    for g in range(2)
                ],
                axis=1,
            )
            picked = lax.dot_general(picker, values, DN_NT, preferred_element_type=jnp.float32)
            picked = picked.reshape(n_block, 8, 2 * half)
            for a in range(2):
                cols[a, :, pair * 8 : (pair + 1) * 8, side * half : (side + 1) * half] = picked[:, :, a * half : (a + 1) * half]

    table = table_ref[...]
    rows = lax.broadcasted_iota(jnp.int32, (n_slot, table.shape[0]), 1).astype(jnp.float32)
    for b in range(n_block):
        spot = pl.ds(b * 128, 128)
        state = jnp.concatenate([near_ref[:, spot], far_ref[:, spot]], axis=0)
        anom = cols[0, b].astype(jnp.bfloat16)
        innov = cols[1, b].astype(jnp.bfloat16)
        inner = jnp.dot(anom, state, preferred_element_type=jnp.float32)
        chooser = jnp.where(rows == prof_ids_ref[:, b : b + 1], 1.0, 0.0).astype(jnp.bfloat16)
        weight = jnp.dot(chooser, table, preferred_element_type=jnp.float32)
        coef = (weight * inner / (M - 1)).astype(jnp.bfloat16)
        corr = lax.dot_general(innov, coef, DN_TN, preferred_element_type=jnp.float32)
        new = (state.astype(jnp.float32) + corr).astype(jnp.bfloat16)
        out_near[:, spot] = new[:half]
        out_far[:, spot] = new[half:]


def run_update(data, near, far, ids, prof_ids, table):
    half, width = near.shape
    n_block = width // 128
    n_slot = prof_ids.shape[0]
    whole = pl.BlockSpec(memory_space=pltpu.VMEM)
    return pl.pallas_call(
        update_kernel,
        out_shape=[jax.ShapeDtypeStruct(near.shape, jnp.bfloat16)] * 2,
        in_specs=[whole] * 21,
        out_specs=[whole] * 2,
        scratch_shapes=[pltpu.VMEM((2, n_block, n_slot, 2 * half), jnp.float32)],
        compiler_params=pltpu.CompilerParams(vmem_limit_bytes=40 * 1024 * 1024),
        cost_estimate=pl.CostEstimate(flops=800_000_000, bytes_accessed=6_500_000, transcendentals=0),
        name="update",
    )(*data, near, far, ids, prof_ids, table)


def x_shift(s):
    return [(x * 2 + c, ((x + s) % X) * 2 + c) for x in range(X) for c in range(2)]


def line(y, z):
    return (y * 4 + z % 4) * 2 + z // 4


def y_shift(s):
    return [(line(y, z), line((y + s) % Y, z)) for y in range(Y) for z in range(Z)]


Z_RUNS = [[line(y, z) for z in range(Z)] for y in range(Y)]
CORE_SWAP = [(i, i ^ 1) for i in range(2 * X)]
SHIFTS = (1, 3, 2)
PLANE = ("cell", "dp")


def shifted(piece, axis, shift):
    out = [piece] + [None] * 3
    for s in SHIFTS:
        out[s] = lax.ppermute(piece, axis, shift(s))
    return out


def local(ensemble, data_anom, weighted_innov, profiles, seg_data, seg_profile):
    n_group = lax.axis_size("cell") * lax.axis_size("dp")
    n_mem = lax.axis_size("mem")
    me_cell, me_dp, me_mem = (lax.axis_index(n) for n in ("cell", "dp", "mem"))
    me_x, me_core = me_mem // 2, me_mem % 2
    me_y, me_zlo = me_cell // 4, me_cell % 4
    mem_dev, cells_dev = ensemble.shape
    data_dev = data_anom.shape[1]
    per_group, blocks = seg_data.shape
    own_blocks = blocks // (n_group * n_mem)
    half_cells = cells_dev // 2
    x_cells = half_cells // X
    own_cells = x_cells // 2

    group = me_cell * 2 + me_dp
    pair_ids = jnp.where(seg_data >= 0, seg_data - group * data_dev + (me_zlo % 2) * data_dev, EMPTY)

    def mine(seg):
        seg = seg.reshape(per_group, n_group, n_mem * own_blocks)
        return lax.dynamic_slice_in_dim(seg, me_mem * own_blocks, own_blocks, 2)

    seg = jnp.stack([mine(pair_ids), mine(seg_profile)]).astype(jnp.bfloat16)
    seg = seg.reshape(2, per_group, Y, Z // 2, 2, own_blocks).transpose(4, 3, 2, 0, 1, 5)
    seg = seg.reshape(Z, Y, 2 * per_group * own_blocks)
    seg = jnp.pad(seg, ((0, 0), (0, 8 - Y), (0, 0)))
    sent = jnp.concatenate(
        [
            jnp.broadcast_to(data_anom[None], (Z,) + data_anom.shape),
            seg,
            jnp.broadcast_to(weighted_innov[None], (Z,) + weighted_innov.shape),
        ],
        axis=1,
    )
    got = lax.all_to_all(sent, PLANE, 0, 0, tiled=True, axis_index_groups=Z_RUNS)

    def state_for(s):
        x_to = (me_x + s) % X
        return lax.dynamic_slice_in_dim(ensemble, me_dp * half_cells + x_to * x_cells, x_cells, 1)

    pieces = [state_for(0)] + [None] * 3
    for s in SHIFTS:
        pieces[s] = lax.ppermute(state_for(s), "mem", x_shift(s))
    state = jnp.concatenate(pieces, axis=0)
    near = lax.dynamic_slice_in_dim(state, me_core * own_cells, own_cells, 1)
    far = lax.ppermute(
        lax.dynamic_slice_in_dim(state, (1 - me_core) * own_cells, own_cells, 1), "mem", CORE_SWAP
    )

    anom_mid = shifted(got[:, : mem_dev + 8], PLANE, y_shift)
    innov_mid = shifted(got[:, mem_dev + 8 :], "mem", x_shift)
    anom_near = shifted(jnp.stack([p[:, :mem_dev] for p in anom_mid]), "mem", x_shift)
    innov_near = shifted(jnp.stack(innov_mid), PLANE, y_shift)
    anom_far = [lax.ppermute(p, "mem", CORE_SWAP) for p in anom_near]
    innov_far = [lax.ppermute(p, "mem", CORE_SWAP) for p in innov_near]

    got_seg = jnp.stack([lax.dynamic_slice_in_dim(p, mem_dev + me_y, 1, 1) for p in anom_mid])
    got_seg = got_seg.astype(jnp.float32).reshape(n_group, 2, per_group, own_blocks)
    ids = got_seg[:, 0].reshape(n_group // 2, 2 * per_group, own_blocks).transpose(2, 1, 0)
    ids = ids.reshape(own_blocks * 2 * per_group, n_group // 2)
    prof_ids = got_seg[:, 1].reshape(n_group * per_group, own_blocks)

    data = anom_near + anom_far + innov_near + innov_far
    new_near, new_far = run_update(data, near, far, ids, prof_ids, profiles)

    back_far = lax.ppermute(new_far, "mem", CORE_SWAP)
    first = me_core == 0
    new = jnp.concatenate([jnp.where(first, new_near, back_far), jnp.where(first, back_far, new_near)], axis=1)
    out = jnp.zeros((mem_dev, half_cells), jnp.bfloat16)
    for s in (0, 2, 1, 3):
        piece = new[s * mem_dev : (s + 1) * mem_dev]
        if s:
            piece = lax.ppermute(piece, "mem", x_shift(X - s))
        out = lax.dynamic_update_slice_in_dim(out, piece, ((me_x + s) % X) * x_cells, 1)
    return out


def solution(mesh):
    placed = (
        P("mem", "cell"),
        P("mem", ("cell", "dp")),
        P("mem", ("cell", "dp")),
        P(),
        P(("cell", "dp"), None),
        P(("cell", "dp"), None),
    )
    return jax.shard_map(
        local, mesh=mesh, in_specs=placed, out_specs=P("mem", ("cell", "dp")), check_vma=False
    )
```

```python
import jax
import jax.numpy as jnp
from jax import lax
from jax.experimental import pallas as pl
from jax.experimental.pallas import tpu as pltpu
from jax.sharding import PartitionSpec as P

M = 256
EMPTY = 512
X, Y, Z = 4, 4, 8
LIST_ROWS = 16
DN_NT = (((1,), (1,)), ((), ()))
DN_TN = (((0,), (0,)), ((), ()))


def update_kernel(*refs):
    n_side = Y + 1
    n_data = 2 * n_side
    data_hbm, (near_hbm, far_hbm, table_ref) = refs[:n_data], refs[n_data : n_data + 3]
    out_near, out_far, data, state, cols, weights, sems, state_sems = refs[n_data + 3 :]
    data_rows = data.shape[3] - LIST_ROWS
    mem_dev = data_rows // (2 * X)
    data_dev = data.shape[4]
    half = X * mem_dev
    n_block = near_hbm.shape[1] // 128

    loads = {}
    for t in range(n_side):
        for side in range(2):
            if t < 2:
                dst = data.at[side, t]
            elif t < 4:
                dst = data.at[side, 2, pl.ds((t - 2) * (Z // 2), Z // 2)]
            else:
                dst = data.at[side, 3]
            loads[side, t] = pltpu.make_async_copy(data_hbm[side * n_side + t], dst, sems.at[side, t])
            loads[side, t].start()
    state_loads = [pltpu.make_async_copy(src, state.at[i], state_sems.at[i]) for i, src in enumerate((near_hbm, far_hbm))]
    for load in state_loads:
        load.start()
    for load in loads.values():
        load.wait()

    me_cell = lax.axis_index("cell")
    me_row = lax.axis_index("dp") * Y + lax.div(me_cell, 4)
    list_rows = lax.broadcasted_iota(jnp.int32, (LIST_ROWS, 128), 0)
    lists = []
    for g in range(2):
        for pair in range(Y * Z // 2):
            t, j = pair // (Z // 2), 2 * (pair % (Z // 2)) + g
            rows = data[0, t, j, data_rows : data_rows + LIST_ROWS].astype(jnp.float32)
            lists.append(jnp.sum(jnp.where(list_rows == me_row, rows, 0.0), axis=0, keepdims=True))
    lists = jnp.concatenate(lists + [jnp.zeros((128 - Y * Z, 128), jnp.float32)], axis=0).T
    later = pltpu.roll(lists, 128 - 2 * Z, 1)
    is_first = lax.rem(lax.broadcasted_iota(jnp.int32, (128, 128), 0), 8) < 4
    ids = jnp.where(is_first, lists, pltpu.roll(later, 4, 0) + data_dev)
    prof_ids = jnp.where(is_first, pltpu.roll(lists, 124, 0), later)

    table = table_ref[...]
    lanes = lax.broadcasted_iota(jnp.int32, (128, 2 * data_dev), 1).astype(jnp.float32)
    prof_lanes = lax.broadcasted_iota(jnp.int32, (128, table.shape[0]), 1).astype(jnp.float32)
    for pair in range(Y * Z // 2):
        t, q = pair // (Z // 2), pair % (Z // 2)
        place = slice(pair * 8, (pair + 1) * 8)
        chooser = jnp.where(prof_lanes == prof_ids[:, pair : pair + 1], 1.0, 0.0).astype(jnp.bfloat16)
        weight = jnp.dot(chooser, table, preferred_element_type=jnp.float32)
        weights[:, place] = weight.reshape(n_block, 8, 128)
        picker = jnp.where(lanes == ids[:, pair : pair + 1], 1.0, 0.0).astype(jnp.bfloat16)
        for side in range(2):
            values = jnp.concatenate(
                [
                    jnp.concatenate(
                        [
                            data[side, t, 2 * q + g, (2 * s + a) * mem_dev : (2 * s + a + 1) * mem_dev]
                            for a in range(2)
                            for s in range(X)
                        ],
                        axis=0,
                    )
                    for g in range(2)
                ],
                axis=1,
            )
            picked = lax.dot_general(picker, values, DN_NT, preferred_element_type=jnp.float32)
            picked = picked.reshape(n_block, 8, 2 * half)
            for a in range(2):
                cols[a, :, place, side * half : (side + 1) * half] = picked[:, :, a * half : (a + 1) * half]

    for load in state_loads:
        load.wait()
    for b in range(n_block):
        spot = pl.ds(b * 128, 128)
        own = jnp.concatenate([state[0, :, spot], state[1, :, spot]], axis=0)
        anom = cols[0, b].astype(jnp.bfloat16)
        innov = cols[1, b].astype(jnp.bfloat16)
        inner = jnp.dot(anom, own, preferred_element_type=jnp.float32)
        coef = (weights[b] * inner / (M - 1)).astype(jnp.bfloat16)
        corr = lax.dot_general(innov, coef, DN_TN, preferred_element_type=jnp.float32)
        new = (own.astype(jnp.float32) + corr).astype(jnp.bfloat16)
        out_near[:, spot] = new[:half]
        out_far[:, spot] = new[half:]


def run_update(data, near, far, table):
    half, width = near.shape
    n_block = width // 128
    n_slot = Y * Z * 4
    any_space = pl.BlockSpec(memory_space=pl.ANY)
    whole = pl.BlockSpec(memory_space=pltpu.VMEM)
    return pl.pallas_call(
        update_kernel,
        out_shape=[jax.ShapeDtypeStruct(near.shape, jnp.bfloat16)] * 2,
        in_specs=[any_space] * (len(data) + 2) + [whole],
        out_specs=[whole] * 2,
        scratch_shapes=[
            pltpu.VMEM((2, Y) + data[0].shape, jnp.bfloat16),
            pltpu.VMEM((2,) + near.shape, jnp.bfloat16),
            pltpu.VMEM((2, n_block, n_slot, 2 * half), jnp.float32),
            pltpu.VMEM((n_block, n_slot, 128), jnp.float32),
            pltpu.SemaphoreType.DMA((2, Y + 1)),
            pltpu.SemaphoreType.DMA((2,)),
        ],
        compiler_params=pltpu.CompilerParams(vmem_limit_bytes=24 * 1024 * 1024),
        cost_estimate=pl.CostEstimate(flops=800_000_000, bytes_accessed=6_500_000, transcendentals=0),
        name="update",
    )(*data, near, far, table)


def line(y, z):
    return (y * 4 + z % 4) * 2 + z // 4


X_SHIFT = [[(x * 2 + c, ((x + s) % X) * 2 + c) for x in range(X) for c in range(2)] for s in range(X)]
Y_SHIFT = [[(line(y, z), line((y + s) % Y, z)) for y in range(Y) for z in range(Z)] for s in range(Y)]
Z_SHIFT = [[(line(y, z), line(y, (z + s) % Z)) for y in range(Y) for z in range(Z)] for s in range(Z)]
CORE_SWAP = [(i, i ^ 1) for i in range(2 * X)]


def to_x(piece, s):
    return lax.ppermute(piece, "mem", X_SHIFT[s % X])


def to_y(piece, s):
    return lax.ppermute(piece, ("cell", "dp"), Y_SHIFT[s % Y])


def to_z(piece, s):
    return lax.ppermute(piece, ("cell", "dp"), Z_SHIFT[s % Z])


def swap(piece):
    return lax.ppermute(piece, "mem", CORE_SWAP)


def after(piece, other):
    return lax.optimization_barrier((piece, other))[0]


def local(ensemble, data_anom, weighted_innov, profiles, seg_data, seg_profile):
    n_group = lax.axis_size("cell") * lax.axis_size("dp")
    n_mem = lax.axis_size("mem")
    me_cell, me_dp, me_mem = (lax.axis_index(n) for n in ("cell", "dp", "mem"))
    me_x, me_core = me_mem // 2, me_mem % 2
    mem_dev, cells_dev = ensemble.shape
    data_dev = data_anom.shape[1]
    per_group, blocks = seg_data.shape
    own_blocks = blocks // (n_group * n_mem)
    half_cells = cells_dev // 2
    x_cells = half_cells // X
    own_cells = x_cells // 2

    own = lax.optimization_barrier(jnp.concatenate([data_anom, weighted_innov], axis=0))
    by_x = [own] + [None] * 3
    for s in (2, 1, 3):
        by_x[s] = to_x(own, s)

    def mine(seg):
        seg = seg.reshape(per_group, n_group, n_mem * own_blocks)
        return lax.dynamic_slice_in_dim(seg, me_mem * own_blocks, own_blocks, 2)

    group = me_cell * 2 + me_dp
    local_ids = jnp.where(seg_data >= 0, seg_data - group * data_dev, EMPTY)
    lists = jnp.stack([mine(local_ids), mine(seg_profile)]).astype(jnp.bfloat16)
    lists = lists.reshape(2, per_group, Y, Z, own_blocks).transpose(3, 2, 4, 0, 1)
    lists = lists.reshape(n_group, own_blocks * 2 * per_group)
    lists = jnp.pad(lists, ((0, LIST_ROWS - 8), (0, 0)))

    unit = jnp.concatenate(by_x + [lists], axis=0)
    data_rows = 2 * mem_dev * X
    by_z = [unit] + [None] * (Z - 1)
    for s in (4, 3, 5, 2, 6, 1, 7):
        by_z[s] = to_z(unit, s)
    first_row = data_rows + (me_cell % 4) * 8
    unit = jnp.stack(
        [
            jnp.concatenate([p[:data_rows], lax.dynamic_slice_in_dim(p, first_row, LIST_ROWS, 0)], axis=0)
            for p in by_z
        ]
    )

    up, down = to_y(unit, 1), to_y(unit, -1)
    up2, down2 = to_y(up[: Z // 2], 1), to_y(down[Z // 2 :], -1)
    data_near = [unit, up, up2, down2, down]
    data_far = [swap(d) for d in data_near]

    def state_for(s):
        x_to = (me_x + s) % X
        return lax.dynamic_slice_in_dim(ensemble, me_dp * half_cells + x_to * x_cells, x_cells, 1)

    pieces = [state_for(0)] + [None] * 3
    last = by_x[2]
    for s in (2, 1, 3):
        pieces[s] = last = to_x(after(state_for(s), last), s)
    state = jnp.concatenate(pieces, axis=0)
    near = lax.dynamic_slice_in_dim(state, me_core * own_cells, own_cells, 1)
    far = swap(lax.dynamic_slice_in_dim(state, (1 - me_core) * own_cells, own_cells, 1))

    new_near, new_far = run_update(data_near + data_far, near, far, profiles)

    back_far = swap(new_far)
    first = me_core == 0
    new = jnp.concatenate([jnp.where(first, new_near, back_far), jnp.where(first, back_far, new_near)], axis=1)
    out = jnp.zeros((mem_dev, half_cells), jnp.bfloat16)
    for s in (0, 2, 1, 3):
        piece = new[s * mem_dev : (s + 1) * mem_dev]
        if s:
            piece = to_x(piece, -s)
        out = lax.dynamic_update_slice_in_dim(out, piece, ((me_x + s) % X) * x_cells, 1)
    return out


def solution(mesh):
    placed = (
        P("mem", "cell"),
        P("mem", ("cell", "dp")),
        P("mem", ("cell", "dp")),
        P(),
        P(("cell", "dp"), None),
        P(("cell", "dp"), None),
    )
    return jax.shard_map(
        local, mesh=mesh, in_specs=placed, out_specs=P("mem", ("cell", "dp")), check_vma=False
    )
```

```python
import jax
import jax.numpy as jnp
from jax import lax
from jax.experimental import pallas as pl
from jax.experimental.pallas import tpu as pltpu
from jax.sharding import PartitionSpec as P

M = 256
EMPTY = 512
X, GROUPS = 4, 32
LIST_ROWS = 8
DN_NT = (((1,), (1,)), ((), ()))
DN_TN = (((0,), (0,)), ((), ()))


def prepare_kernel(anom_hbm, innov_hbm, seg_hbm, prof_hbm, sent_ref, data, lists, sems):
    sources = (anom_hbm, innov_hbm, seg_hbm, prof_hbm)
    targets = (data.at[0], data.at[1], lists.at[0], lists.at[1])
    loads = [pltpu.make_async_copy(src, dst, sems.at[i]) for i, (src, dst) in enumerate(zip(sources, targets))]
    for load in loads:
        load.start()
    me_cell, me_dp, me_mem = (lax.axis_index(n) for n in ("cell", "dp", "mem"))
    _, mem_dev, data_dev = data.shape
    per_group = lists.shape[1]
    per_block = 2 * per_group
    own_blocks = 128 // per_block

    lane_in = lax.broadcasted_iota(jnp.int32, (128, 128), 0)
    lane_out = lax.broadcasted_iota(jnp.int32, (128, 128), 1)
    select = lane_in == me_mem * own_blocks + lax.rem(lane_out, own_blocks)
    select = jnp.where(select, 1.0, 0.0).astype(jnp.bfloat16)
    for load in loads[2:]:
        load.wait()
    ids = lists[0]
    ids = jnp.where(ids >= 0, ids - (me_cell * 2 + me_dp) * data_dev, EMPTY)
    both = jnp.concatenate([ids, lists[1]], axis=0).astype(jnp.float32)
    tiles = [both[:, g * 128 : (g + 1) * 128] for g in range(GROUPS)]
    spread = jnp.dot(jnp.concatenate(tiles, axis=0).astype(jnp.bfloat16), select, preferred_element_type=jnp.float32)
    shape = (GROUPS, per_block, 128)
    kept = lax.broadcasted_iota(jnp.int32, shape, 1) == lax.div(lax.broadcasted_iota(jnp.int32, shape, 2), own_blocks)
    packed = jnp.sum(jnp.where(kept, spread.reshape(shape), 0.0), axis=1)
    for load in loads[:2]:
        load.wait()
    block = jnp.concatenate([data[0], data[1]], axis=0)
    filler = jnp.zeros((LIST_ROWS - 1, 128), jnp.float32)
    for g in range(GROUPS):
        rows = jnp.concatenate([packed[g : g + 1], filler], axis=0).astype(jnp.bfloat16)
        sent_ref[g] = jnp.concatenate([block, rows], axis=0)


def prepare(anom, innov, seg, prof):
    mem_dev, data_dev = anom.shape
    return pl.pallas_call(
        prepare_kernel,
        out_shape=jax.ShapeDtypeStruct((GROUPS, 2 * mem_dev + LIST_ROWS, data_dev), jnp.bfloat16),
        in_specs=[pl.BlockSpec(memory_space=pl.ANY)] * 4,
        out_specs=pl.BlockSpec(memory_space=pltpu.VMEM),
        scratch_shapes=[
            pltpu.VMEM((2,) + anom.shape, jnp.bfloat16),
            pltpu.VMEM((2,) + seg.shape, jnp.int32),
            pltpu.SemaphoreType.DMA((4,)),
        ],
        compiler_params=pltpu.CompilerParams(vmem_limit_bytes=60 * 1024 * 1024),
        cost_estimate=pl.CostEstimate(flops=10_000_000, bytes_accessed=400_000, transcendentals=0),
        name="prepare",
    )(anom, innov, seg, prof)


def update_kernel(*refs):
    n_side = X + 1
    n_data = 2 * n_side
    data_hbm, (near_hbm, far_hbm, lists_ref, table_ref) = refs[:n_data], refs[n_data : n_data + 4]
    out_near, out_far, data, state, cols, weights, sems, state_sems = refs[n_data + 4 :]
    mem_dev = data.shape[3] // 2
    data_dev = data.shape[4]
    half = X * mem_dev
    n_block = near_hbm.shape[1] // 128

    loads = {}
    for s in range(n_side):
        for side in range(2):
            if s < 2:
                dst = data.at[side, s]
            elif s < 4:
                dst = data.at[side, 2, pl.ds((s - 2) * (GROUPS // 2), GROUPS // 2)]
            else:
                dst = data.at[side, 3]
            loads[side, s] = pltpu.make_async_copy(data_hbm[side * n_side + s], dst, sems.at[side, s])
            loads[side, s].start()
    state_loads = [pltpu.make_async_copy(src, state.at[i], state_sems.at[i]) for i, src in enumerate((near_hbm, far_hbm))]
    for load in state_loads:
        load.start()

    row = lax.broadcasted_iota(jnp.int32, (128, 128), 0)
    lane = lax.broadcasted_iota(jnp.int32, (128, 128), 1)
    order = jnp.where(lane == lax.rem(row, 8) * n_block + lax.div(row, 8), 1.0, 0.0).astype(jnp.bfloat16)
    lists = jnp.concatenate([lists_ref[...], jnp.zeros((128 - GROUPS, 128), jnp.bfloat16)], axis=0)
    lists = lax.dot_general(order, lists, DN_NT, preferred_element_type=jnp.float32)
    later = pltpu.roll(lists, 127, 1)
    is_first = lax.rem(lax.broadcasted_iota(jnp.int32, (128, 128), 0), 8) < 4
    ids = jnp.where(is_first, lists, pltpu.roll(later, 4, 0) + data_dev)
    prof_ids = jnp.where(is_first, pltpu.roll(lists, 124, 0), later)

    table = table_ref[...]
    lanes = lax.broadcasted_iota(jnp.int32, (128, 2 * data_dev), 1).astype(jnp.float32)
    prof_lanes = lax.broadcasted_iota(jnp.int32, (128, table.shape[0]), 1).astype(jnp.float32)
    for load in loads.values():
        load.wait()
    for pair in range(GROUPS // 2):
        column = slice(2 * pair, 2 * pair + 1)
        place = slice(pair * 8, (pair + 1) * 8)
        chooser = jnp.where(prof_lanes == prof_ids[:, column], 1.0, 0.0).astype(jnp.bfloat16)
        weight = jnp.dot(chooser, table, preferred_element_type=jnp.float32)
        weights[:, place] = weight.reshape(n_block, 8, 128)
        picker = jnp.where(lanes == ids[:, column], 1.0, 0.0).astype(jnp.bfloat16)
        for side in range(2):
            values = jnp.concatenate(
                [
                    jnp.concatenate(
                        [
                            data[side, s, 2 * pair + g, a * mem_dev : (a + 1) * mem_dev]
                            for a in range(2)
                            for s in range(X)
                        ],
                        axis=0,
                    )
                    for g in range(2)
                ],
                axis=1,
            )
            picked = lax.dot_general(picker, values, DN_NT, preferred_element_type=jnp.float32)
            picked = picked.reshape(n_block, 8, 2 * half)
            for a in range(2):
                cols[a, :, place, side * half : (side + 1) * half] = picked[:, :, a * half : (a + 1) * half]

    for load in state_loads:
        load.wait()
    for b in range(n_block):
        spot = pl.ds(b * 128, 128)
        own = jnp.concatenate([state[0, :, spot], state[1, :, spot]], axis=0)
        anom = cols[0, b].astype(jnp.bfloat16)
        innov = cols[1, b].astype(jnp.bfloat16)
        inner = jnp.dot(anom, own, preferred_element_type=jnp.float32)
        coef = (weights[b] * inner / (M - 1)).astype(jnp.bfloat16)
        corr = lax.dot_general(innov, coef, DN_TN, preferred_element_type=jnp.float32)
        new = (own.astype(jnp.float32) + corr).astype(jnp.bfloat16)
        out_near[:, spot] = new[:half]
        out_far[:, spot] = new[half:]


def run_update(data, near, far, lists, table):
    half, width = near.shape
    n_block = width // 128
    n_slot = GROUPS * 4
    any_space = pl.BlockSpec(memory_space=pl.ANY)
    whole = pl.BlockSpec(memory_space=pltpu.VMEM)
    return pl.pallas_call(
        update_kernel,
        out_shape=[jax.ShapeDtypeStruct(near.shape, jnp.bfloat16)] * 2,
        in_specs=[any_space] * (len(data) + 2) + [whole] * 2,
        out_specs=[whole] * 2,
        scratch_shapes=[
            pltpu.VMEM((2, X) + data[0].shape, jnp.bfloat16),
            pltpu.VMEM((2,) + near.shape, jnp.bfloat16),
            pltpu.VMEM((2, n_block, n_slot, 2 * half), jnp.float32),
            pltpu.VMEM((n_block, n_slot, 128), jnp.float32),
            pltpu.SemaphoreType.DMA((2, X + 1)),
            pltpu.SemaphoreType.DMA((2,)),
        ],
        compiler_params=pltpu.CompilerParams(vmem_limit_bytes=24 * 1024 * 1024),
        cost_estimate=pl.CostEstimate(flops=800_000_000, bytes_accessed=6_500_000, transcendentals=0),
        name="update",
    )(*data, near, far, lists, table)


X_SHIFT = [[(x * 2 + c, ((x + s) % X) * 2 + c) for x in range(X) for c in range(2)] for s in range(X)]
CORE_SWAP = [(i, i ^ 1) for i in range(2 * X)]


def to_x(piece, s):
    return lax.ppermute(piece, "mem", X_SHIFT[s % X])


def swap(piece):
    return lax.ppermute(piece, "mem", CORE_SWAP)


def local(ensemble, data_anom, weighted_innov, profiles, seg_data, seg_profile):
    me_dp, me_mem = lax.axis_index("dp"), lax.axis_index("mem")
    me_x, me_core = me_mem // 2, me_mem % 2
    mem_dev, cells_dev = ensemble.shape
    half_cells = cells_dev // 2
    x_cells = half_cells // X
    own_cells = x_cells // 2

    sent = prepare(data_anom, weighted_innov, seg_data, seg_profile)
    got = lax.all_to_all(sent, ("cell", "dp"), 0, 0, tiled=True)

    def state_for(s):
        x_to = (me_x + s) % X
        return lax.dynamic_slice_in_dim(ensemble, me_dp * half_cells + x_to * x_cells, x_cells, 1)

    pieces = [state_for(0)] + [None] * 3
    for s in (2, 1, 3):
        pieces[s] = to_x(state_for(s), s)
    state = jnp.concatenate(pieces, axis=0)
    near = lax.dynamic_slice_in_dim(state, me_core * own_cells, own_cells, 1)
    far = swap(lax.dynamic_slice_in_dim(state, (1 - me_core) * own_cells, own_cells, 1))

    data_rows = 2 * mem_dev
    own, lists = got[:, :data_rows], got[:, data_rows]
    up, down = to_x(own, 1), to_x(own, -1)
    up2, down2 = to_x(up[: GROUPS // 2], 1), to_x(down[GROUPS // 2 :], -1)
    data_near = [own, up, up2, down2, down]
    data_far = [swap(d) for d in data_near]

    new_near, new_far = run_update(data_near + data_far, near, far, lists, profiles)

    back_far = swap(new_far)
    first = me_core == 0
    new = jnp.concatenate([jnp.where(first, new_near, back_far), jnp.where(first, back_far, new_near)], axis=1)
    out = jnp.zeros((mem_dev, half_cells), jnp.bfloat16)
    for s in (0, 2, 1, 3):
        piece = new[s * mem_dev : (s + 1) * mem_dev]
        if s:
            piece = to_x(piece, -s)
        out = lax.dynamic_update_slice_in_dim(out, piece, ((me_x + s) % X) * x_cells, 1)
    return out


def solution(mesh):
    placed = (
        P("mem", "cell"),
        P("mem", ("cell", "dp")),
        P("mem", ("cell", "dp")),
        P(),
        P(("cell", "dp"), None),
        P(("cell", "dp"), None),
    )
    return jax.shard_map(
        local, mesh=mesh, in_specs=placed, out_specs=P("mem", ("cell", "dp")), check_vma=False
    )
```

```python
import jax
import jax.numpy as jnp
from jax import lax
from jax.experimental import pallas as pl
from jax.experimental.pallas import tpu as pltpu
from jax.sharding import PartitionSpec as P

M = 256
EMPTY = 512
X, Y, Z, GROUPS = 4, 4, 8, 32
LIST_ROWS = 8
DN_NT = (((1,), (1,)), ((), ()))
DN_TN = (((0,), (0,)), ((), ()))


def prepare_kernel(anom_hbm, innov_hbm, seg_hbm, prof_hbm, sent_ref, data, lists, sems):
    sources = (anom_hbm, innov_hbm, seg_hbm, prof_hbm)
    targets = (data.at[0], data.at[1], lists.at[0], lists.at[1])
    loads = [pltpu.make_async_copy(src, dst, sems.at[i]) for i, (src, dst) in enumerate(zip(sources, targets))]
    for load in loads:
        load.start()
    me_cell, me_dp, me_mem = (lax.axis_index(n) for n in ("cell", "dp", "mem"))
    _, mem_dev, data_dev = data.shape
    per_group = lists.shape[1]
    per_block = 2 * per_group
    own_blocks = 128 // per_block

    lane_in = lax.broadcasted_iota(jnp.int32, (128, 256), 0)
    lane_out = lax.broadcasted_iota(jnp.int32, (128, 256), 1)
    start = lax.div(me_mem, 2) * 2 * own_blocks + lax.div(lane_out, 128) * own_blocks
    select = jnp.where(lane_in == start + lax.rem(lane_out, own_blocks), 1.0, 0.0).astype(jnp.bfloat16)
    for load in loads[2:]:
        load.wait()
    ids = lists[0]
    ids = jnp.where(ids >= 0, ids - (me_cell * 2 + me_dp) * data_dev, EMPTY)
    both = jnp.concatenate([ids, lists[1]], axis=0).astype(jnp.float32)
    tiles = [both[:, g * 128 : (g + 1) * 128] for g in range(GROUPS)]
    spread = jnp.dot(jnp.concatenate(tiles, axis=0).astype(jnp.bfloat16), select, preferred_element_type=jnp.float32)
    shape = (GROUPS, per_block, 256)
    lane_out = lax.rem(lax.broadcasted_iota(jnp.int32, shape, 2), 128)
    kept = lax.broadcasted_iota(jnp.int32, shape, 1) == lax.div(lane_out, own_blocks)
    packed = jnp.sum(jnp.where(kept, spread.reshape(shape), 0.0), axis=1)
    for load in loads[:2]:
        load.wait()
    block = jnp.concatenate([data[0], data[1]], axis=0)
    filler = jnp.zeros((LIST_ROWS - 2, 128), jnp.float32)
    for g in range(GROUPS):
        rows = jnp.concatenate([packed[g : g + 1, :128], packed[g : g + 1, 128:], filler], axis=0).astype(jnp.bfloat16)
        sent_ref[g] = jnp.concatenate([block, rows], axis=0)


def prepare(anom, innov, seg, prof):
    mem_dev, data_dev = anom.shape
    return pl.pallas_call(
        prepare_kernel,
        out_shape=jax.ShapeDtypeStruct((GROUPS, 2 * mem_dev + LIST_ROWS, data_dev), jnp.bfloat16),
        in_specs=[pl.BlockSpec(memory_space=pl.ANY)] * 4,
        out_specs=pl.BlockSpec(memory_space=pltpu.VMEM),
        scratch_shapes=[
            pltpu.VMEM((2,) + anom.shape, jnp.bfloat16),
            pltpu.VMEM((2,) + seg.shape, jnp.int32),
            pltpu.SemaphoreType.DMA((4,)),
        ],
        compiler_params=pltpu.CompilerParams(vmem_limit_bytes=60 * 1024 * 1024),
        cost_estimate=pl.CostEstimate(flops=10_000_000, bytes_accessed=400_000, transcendentals=0),
        name="prepare",
    )(anom, innov, seg, prof)


def update_kernel(*refs):
    data = (refs[:X], refs[X : 2 * X])
    near_hbm, far_hbm, lists_near, lists_far, table_ref = refs[2 * X : 2 * X + 5]
    out_near, out_far, state, cols, weights, columns, state_sems = refs[2 * X + 5 :]
    half = near_hbm.shape[0]
    mem_dev = half // X
    data_dev = refs[0].shape[2]
    n_block = near_hbm.shape[1] // 128

    state_loads = [pltpu.make_async_copy(src, state.at[i], state_sems.at[i]) for i, src in enumerate((near_hbm, far_hbm))]
    for load in state_loads:
        load.start()

    me_y = lax.div(lax.axis_index("cell"), 4)
    me_mem = lax.axis_index("mem")
    me_x, me_core = lax.div(me_mem, 2), lax.rem(me_mem, 2)
    x_at = [lax.rem(me_x - i + X, X) * Z for i in range(X)]
    y_at = [lax.rem(me_y - i + Y, Y) * Z for i in range(Y)]

    row = lax.broadcasted_iota(jnp.int32, (128, 128), 0)
    lane = lax.broadcasted_iota(jnp.int32, (128, 128), 1)
    order = jnp.where(lane == lax.rem(row, 8) * n_block + lax.div(row, 8), 1.0, 0.0).astype(jnp.bfloat16)
    lists = []
    for i in range(Y):
        here = [part[pl.ds(y_at[i], Z)].astype(jnp.float32) for part in (lists_near, lists_far)]
        here = jnp.where(me_core == 0, here[0], here[1])
        wanted = lax.broadcasted_iota(jnp.int32, here.shape, 1) == me_core
        lists.append(jnp.sum(jnp.where(wanted, here, 0.0), axis=1))
    lists = jnp.concatenate(lists + [jnp.zeros((128 - GROUPS, 128), jnp.float32)], axis=0).astype(jnp.bfloat16)
    lists = lax.dot_general(order, lists, DN_NT, preferred_element_type=jnp.float32)
    later = pltpu.roll(lists, 127, 1)
    is_first = lax.rem(row, 8) < 4
    columns[...] = jnp.where(is_first, lists, pltpu.roll(later, 4, 0) + data_dev)
    prof_ids = jnp.where(is_first, pltpu.roll(lists, 124, 0), later)

    table = table_ref[...]
    prof_lanes = lax.broadcasted_iota(jnp.int32, (128, table.shape[0]), 1).astype(jnp.float32)
    for pair in range(GROUPS // 2):
        chooser = jnp.where(prof_lanes == prof_ids[:, 2 * pair : 2 * pair + 1], 1.0, 0.0).astype(jnp.bfloat16)
        weight = jnp.dot(chooser, table, preferred_element_type=jnp.float32)
        weights[:, pair * 8 : (pair + 1) * 8] = weight.reshape(n_block, 8, 128)

    def select(core):
        lanes = lax.broadcasted_iota(jnp.int32, (128, 2 * data_dev), 1).astype(jnp.float32)
        ids = columns[...]
        for pair in range(GROUPS // 2):
            i, q = pair // (Z // 2), pair % (Z // 2)
            picker = jnp.where(lanes == ids[:, 2 * pair : 2 * pair + 1], 1.0, 0.0).astype(jnp.bfloat16)
            for side in range(2):

                def piece(s, g, a):
                    rows = slice(a * mem_dev, (a + 1) * mem_dev)
                    if side == core:
                        return data[side][s][y_at[i] + 2 * q + g, rows]
                    return data[side][i][x_at[s] + 2 * q + g, rows]

                values = jnp.concatenate(
                    [
                        jnp.concatenate([piece(s, g, a) for a in range(2) for s in range(X)], axis=0)
                        for g in range(2)
                    ],
                    axis=1,
                )
                picked = lax.dot_general(picker, values, DN_NT, preferred_element_type=jnp.float32)
                picked = picked.reshape(n_block, 8, 2 * half)
                for a in range(2):
                    cols[a, :, pair * 8 : (pair + 1) * 8, side * half : (side + 1) * half] = picked[:, :, a * half : (a + 1) * half]

    for core in range(2):
        pl.when(me_core == core)(lambda core=core: select(core))

    for load in state_loads:
        load.wait()
    for b in range(n_block):
        spot = pl.ds(b * 128, 128)
        own = jnp.concatenate([state[0, :, spot], state[1, :, spot]], axis=0)
        anom = cols[0, b].astype(jnp.bfloat16)
        innov = cols[1, b].astype(jnp.bfloat16)
        inner = jnp.dot(anom, own, preferred_element_type=jnp.float32)
        coef = (weights[b] * inner / (M - 1)).astype(jnp.bfloat16)
        corr = lax.dot_general(innov, coef, DN_TN, preferred_element_type=jnp.float32)
        new = (own.astype(jnp.float32) + corr).astype(jnp.bfloat16)
        out_near[:, spot] = new[:half]
        out_far[:, spot] = new[half:]


def run_update(data, near, far, lists_near, lists_far, table):
    half, width = near.shape
    n_block = width // 128
    n_slot = GROUPS * 4
    any_space = pl.BlockSpec(memory_space=pl.ANY)
    whole = pl.BlockSpec(memory_space=pltpu.VMEM)
    return pl.pallas_call(
        update_kernel,
        out_shape=[jax.ShapeDtypeStruct(near.shape, jnp.bfloat16)] * 2,
        in_specs=[whole] * len(data) + [any_space] * 2 + [whole] * 3,
        out_specs=[whole] * 2,
        scratch_shapes=[
            pltpu.VMEM((2,) + near.shape, jnp.bfloat16),
            pltpu.VMEM((2, n_block, n_slot, 2 * half), jnp.float32),
            pltpu.VMEM((n_block, n_slot, 128), jnp.float32),
            pltpu.VMEM((128, 128), jnp.float32),
            pltpu.SemaphoreType.DMA((2,)),
        ],
        compiler_params=pltpu.CompilerParams(vmem_limit_bytes=16 * 1024 * 1024),
        cost_estimate=pl.CostEstimate(flops=800_000_000, bytes_accessed=6_500_000, transcendentals=0),
        name="update",
    )(*data, near, far, lists_near, lists_far, table)


def device(x, y, z, core):
    return ((y * 4 + z // 2) * 2 * X + x * 2 + core) * 2 + z % 2


X_SHIFT = [[(x * 2 + c, ((x + s) % X) * 2 + c) for x in range(X) for c in range(2)] for s in range(X)]
EVERY = ("cell", "mem", "dp")
PLANES = [[device(x, y, z, 0) for y in range(Y) for z in range(Z)] for x in range(X)]
PLANES += [[device(x, y, z, 1) for x in range(X) for z in range(Z)] for y in range(Y)]
CROSS = [
    [(device(x, y, z, 0), device((x + s) % X, y, z, 0)) for x in range(X) for y in range(Y) for z in range(Z)]
    + [(device(x, y, z, 1), device(x, (y + s) % Y, z, 1)) for x in range(X) for y in range(Y) for z in range(Z)]
    for s in range(X)
]
CORE_SWAP = [(i, i ^ 1) for i in range(2 * X)]


def to_x(piece, s):
    return lax.ppermute(piece, "mem", X_SHIFT[s % X])


def cross(piece, s):
    return lax.ppermute(piece, EVERY, CROSS[s % X])


def after(pieces, others):
    return lax.optimization_barrier((pieces, others))[0]


def swap(piece):
    return lax.ppermute(piece, "mem", CORE_SWAP)


def local(ensemble, data_anom, weighted_innov, profiles, seg_data, seg_profile):
    me_dp, me_mem = lax.axis_index("dp"), lax.axis_index("mem")
    me_x, me_core = me_mem // 2, me_mem % 2
    mem_dev, cells_dev = ensemble.shape
    half_cells = cells_dev // 2
    x_cells = half_cells // X
    own_cells = x_cells // 2

    sent = prepare(data_anom, weighted_innov, seg_data, seg_profile)
    got = lax.all_to_all(sent, EVERY, 0, 0, tiled=True, axis_index_groups=PLANES)

    def state_for(s):
        x_to = (me_x + s) % X
        return lax.dynamic_slice_in_dim(ensemble, me_dp * half_cells + x_to * x_cells, x_cells, 1)

    pieces = [state_for(0)] + [None] * 3
    for s in (2, 1, 3):
        pieces[s] = to_x(state_for(s), s)
    data_rows = 2 * mem_dev
    own = after(got, pieces[1:])[:, :data_rows]
    data_near = [got] + [None] * 3
    for s in (2, 1, 3):
        data_near[s] = cross(own, s)
    data_far = [swap(d) for d in data_near]
    first = me_core == 0
    lists_near, lists_far = got[:, data_rows:], data_far[0][:, data_rows:]

    state = jnp.concatenate(after(pieces, data_near[1]), axis=0)
    near = lax.dynamic_slice_in_dim(state, me_core * own_cells, own_cells, 1)
    far = swap(lax.dynamic_slice_in_dim(state, (1 - me_core) * own_cells, own_cells, 1))

    new_near, new_far = run_update(data_near + data_far, near, far, lists_near, lists_far, profiles)

    across = slice(2 * mem_dev, 3 * mem_dev)
    near2 = to_x(new_near[across], 2)
    back_far = swap(new_far)
    far2 = to_x(back_far[across], 2)
    new = jnp.concatenate([jnp.where(first, new_near, back_far), jnp.where(first, back_far, new_near)], axis=1)
    out = jnp.zeros((mem_dev, half_cells), jnp.bfloat16)

    def place(out, piece, s, start):
        return lax.dynamic_update_slice_in_dim(out, piece, ((me_x + s) % X) * x_cells + start, 1)

    out = place(out, new[:mem_dev], 0, 0)
    backs = [to_x(new[s * mem_dev : (s + 1) * mem_dev], -s) for s in (1, 3)]
    out = place(out, near2, 2, me_core * own_cells)
    out = place(out, far2, 2, (1 - me_core) * own_cells)
    out = place(out, backs[0], 1, 0)
    return place(out, backs[1], 3, 0)


def solution(mesh):
    placed = (
        P("mem", "cell"),
        P("mem", ("cell", "dp")),
        P("mem", ("cell", "dp")),
        P(),
        P(("cell", "dp"), None),
        P(("cell", "dp"), None),
    )
    return jax.shard_map(
        local, mesh=mesh, in_specs=placed, out_specs=P("mem", ("cell", "dp")), check_vma=False
    )
```

```python
import jax
import jax.numpy as jnp
from jax import lax
from jax.experimental import pallas as pl
from jax.experimental.pallas import tpu as pltpu
from jax.sharding import PartitionSpec as P

M = 256
EMPTY = 512
X, Y, Z, GROUPS = 4, 4, 8, 32
LIST_ROWS = 8
DN_NT = (((1,), (1,)), ((), ()))
DN_TN = (((0,), (0,)), ((), ()))


def prepare_kernel(anom_hbm, innov_hbm, seg_hbm, prof_hbm, sent_ref, data, lists, sems):
    sources = (anom_hbm, innov_hbm, seg_hbm, prof_hbm)
    targets = (data.at[0], data.at[1], lists.at[0], lists.at[1])
    loads = [pltpu.make_async_copy(src, dst, sems.at[i]) for i, (src, dst) in enumerate(zip(sources, targets))]
    for load in loads:
        load.start()
    me_cell, me_dp, me_mem = (lax.axis_index(n) for n in ("cell", "dp", "mem"))
    _, mem_dev, data_dev = data.shape
    per_group = lists.shape[1]
    per_block = 2 * per_group
    own_blocks = 128 // per_block

    lane_in = lax.broadcasted_iota(jnp.int32, (128, 256), 0)
    lane_out = lax.broadcasted_iota(jnp.int32, (128, 256), 1)
    start = lax.div(me_mem, 2) * 2 * own_blocks + lax.div(lane_out, 128) * own_blocks
    select = jnp.where(lane_in == start + lax.rem(lane_out, own_blocks), 1.0, 0.0).astype(jnp.bfloat16)
    for load in loads[2:]:
        load.wait()
    ids = lists[0]
    ids = jnp.where(ids >= 0, ids - (me_cell * 2 + me_dp) * data_dev, EMPTY)
    both = jnp.concatenate([ids, lists[1]], axis=0).astype(jnp.float32)
    tiles = [both[:, g * 128 : (g + 1) * 128] for g in range(GROUPS)]
    spread = jnp.dot(jnp.concatenate(tiles, axis=0).astype(jnp.bfloat16), select, preferred_element_type=jnp.float32)
    shape = (GROUPS, per_block, 256)
    lane_out = lax.rem(lax.broadcasted_iota(jnp.int32, shape, 2), 128)
    kept = lax.broadcasted_iota(jnp.int32, shape, 1) == lax.div(lane_out, own_blocks)
    packed = jnp.sum(jnp.where(kept, spread.reshape(shape), 0.0), axis=1)
    for load in loads[:2]:
        load.wait()
    block = jnp.concatenate([data[0], data[1]], axis=0)
    filler = jnp.zeros((LIST_ROWS - 2, 128), jnp.float32)
    for g in range(GROUPS):
        rows = jnp.concatenate([packed[g : g + 1, :128], packed[g : g + 1, 128:], filler], axis=0).astype(jnp.bfloat16)
        sent_ref[g] = jnp.concatenate([block, rows], axis=0)


def prepare(anom, innov, seg, prof):
    mem_dev, data_dev = anom.shape
    return pl.pallas_call(
        prepare_kernel,
        out_shape=jax.ShapeDtypeStruct((GROUPS, 2 * mem_dev + LIST_ROWS, data_dev), jnp.bfloat16),
        in_specs=[pl.BlockSpec(memory_space=pl.ANY)] * 4,
        out_specs=pl.BlockSpec(memory_space=pltpu.VMEM),
        scratch_shapes=[
            pltpu.VMEM((2,) + anom.shape, jnp.bfloat16),
            pltpu.VMEM((2,) + seg.shape, jnp.int32),
            pltpu.SemaphoreType.DMA((4,)),
        ],
        compiler_params=pltpu.CompilerParams(vmem_limit_bytes=60 * 1024 * 1024),
        cost_estimate=pl.CostEstimate(flops=10_000_000, bytes_accessed=400_000, transcendentals=0),
        name="prepare",
    )(anom, innov, seg, prof)


def choose_kernel(lists_near, lists_far, table_ref, picker_ref, weights_ref):
    n_block = weights_ref.shape[0]
    data_dev = picker_ref.shape[2] // 2
    me_y = lax.div(lax.axis_index("cell"), 4)
    me_core = lax.rem(lax.axis_index("mem"), 2)
    y_at = [lax.rem(me_y - i + Y, Y) * Z for i in range(Y)]

    row = lax.broadcasted_iota(jnp.int32, (128, 128), 0)
    lane = lax.broadcasted_iota(jnp.int32, (128, 128), 1)
    order = jnp.where(lane == lax.rem(row, 8) * n_block + lax.div(row, 8), 1.0, 0.0).astype(jnp.bfloat16)
    lists = []
    for i in range(Y):
        here = [part[pl.ds(y_at[i], Z)].astype(jnp.float32) for part in (lists_near, lists_far)]
        here = jnp.where(me_core == 0, here[0], here[1])
        wanted = lax.broadcasted_iota(jnp.int32, here.shape, 1) == me_core
        lists.append(jnp.sum(jnp.where(wanted, here, 0.0), axis=1))
    lists = jnp.concatenate(lists + [jnp.zeros((128 - GROUPS, 128), jnp.float32)], axis=0).astype(jnp.bfloat16)
    lists = lax.dot_general(order, lists, DN_NT, preferred_element_type=jnp.float32)
    later = pltpu.roll(lists, 127, 1)
    is_first = lax.rem(row, 8) < 4
    ids = jnp.where(is_first, lists, pltpu.roll(later, 4, 0) + data_dev)
    prof_ids = jnp.where(is_first, pltpu.roll(lists, 124, 0), later)

    table = table_ref[...]
    prof_lanes = lax.broadcasted_iota(jnp.int32, (128, table.shape[0]), 1).astype(jnp.float32)
    lanes = lax.broadcasted_iota(jnp.int32, (128, picker_ref.shape[2]), 1).astype(jnp.float32)
    for pair in range(GROUPS // 2):
        column = slice(2 * pair, 2 * pair + 1)
        picker_ref[pair] = jnp.where(lanes == ids[:, column], 1.0, 0.0).astype(jnp.bfloat16)
        chooser = jnp.where(prof_lanes == prof_ids[:, column], 1.0, 0.0).astype(jnp.bfloat16)
        weight = jnp.dot(chooser, table, preferred_element_type=jnp.float32)
        weights_ref[:, pair * 8 : (pair + 1) * 8] = weight.reshape(n_block, 8, 128)


def choose(lists_near, lists_far, table, n_block, data_dev):
    whole = pl.BlockSpec(memory_space=pltpu.VMEM)
    n_slot = GROUPS * 4
    return pl.pallas_call(
        choose_kernel,
        out_shape=[
            jax.ShapeDtypeStruct((GROUPS // 2, 8 * n_block, 2 * data_dev), jnp.bfloat16),
            jax.ShapeDtypeStruct((n_block, n_slot, 128), jnp.float32),
        ],
        in_specs=[whole] * 3,
        out_specs=[whole] * 2,
        compiler_params=pltpu.CompilerParams(vmem_limit_bytes=8 * 1024 * 1024),
        cost_estimate=pl.CostEstimate(flops=40_000_000, bytes_accessed=2_300_000, transcendentals=0),
        name="choose",
    )(lists_near, lists_far, table)


def update_kernel(*refs):
    data = (refs[:X], refs[X : 2 * X])
    near_hbm, far_hbm, picker_ref, weights = refs[2 * X : 2 * X + 4]
    out_near, out_far, state, cols, state_sems = refs[2 * X + 4 :]
    half = near_hbm.shape[0]
    mem_dev = half // X
    n_block = near_hbm.shape[1] // 128

    state_loads = [pltpu.make_async_copy(src, state.at[i], state_sems.at[i]) for i, src in enumerate((near_hbm, far_hbm))]
    for load in state_loads:
        load.start()

    me_y = lax.div(lax.axis_index("cell"), 4)
    me_mem = lax.axis_index("mem")
    me_x, me_core = lax.div(me_mem, 2), lax.rem(me_mem, 2)
    x_at = [lax.rem(me_x - i + X, X) * Z for i in range(X)]
    y_at = [lax.rem(me_y - i + Y, Y) * Z for i in range(Y)]

    def select(core):
        for pair in range(GROUPS // 2):
            i, q = pair // (Z // 2), pair % (Z // 2)
            picker = picker_ref[pair]
            for side in range(2):

                def piece(s, g, a):
                    rows = slice(a * mem_dev, (a + 1) * mem_dev)
                    if side == core:
                        return data[side][s][y_at[i] + 2 * q + g, rows]
                    return data[side][i][x_at[s] + 2 * q + g, rows]

                values = jnp.concatenate(
                    [
                        jnp.concatenate([piece(s, g, a) for a in range(2) for s in range(X)], axis=0)
                        for g in range(2)
                    ],
                    axis=1,
                )
                picked = lax.dot_general(picker, values, DN_NT, preferred_element_type=jnp.float32)
                picked = picked.reshape(n_block, 8, 2 * half)
                for a in range(2):
                    cols[a, :, pair * 8 : (pair + 1) * 8, side * half : (side + 1) * half] = picked[:, :, a * half : (a + 1) * half]

    for core in range(2):
        pl.when(me_core == core)(lambda core=core: select(core))

    for load in state_loads:
        load.wait()
    for b in range(n_block):
        spot = pl.ds(b * 128, 128)
        own = jnp.concatenate([state[0, :, spot], state[1, :, spot]], axis=0)
        anom = cols[0, b].astype(jnp.bfloat16)
        innov = cols[1, b].astype(jnp.bfloat16)
        inner = jnp.dot(anom, own, preferred_element_type=jnp.float32)
        coef = (weights[b] * inner / (M - 1)).astype(jnp.bfloat16)
        corr = lax.dot_general(innov, coef, DN_TN, preferred_element_type=jnp.float32)
        new = (own.astype(jnp.float32) + corr).astype(jnp.bfloat16)
        out_near[:, spot] = new[:half]
        out_far[:, spot] = new[half:]


def run_update(data, near, far, picker, weights):
    half, width = near.shape
    n_block = width // 128
    n_slot = GROUPS * 4
    any_space = pl.BlockSpec(memory_space=pl.ANY)
    whole = pl.BlockSpec(memory_space=pltpu.VMEM)
    return pl.pallas_call(
        update_kernel,
        out_shape=[jax.ShapeDtypeStruct(near.shape, jnp.bfloat16)] * 2,
        in_specs=[whole] * len(data) + [any_space] * 2 + [whole] * 2,
        out_specs=[whole] * 2,
        scratch_shapes=[
            pltpu.VMEM((2,) + near.shape, jnp.bfloat16),
            pltpu.VMEM((2, n_block, n_slot, 2 * half), jnp.float32),
            pltpu.SemaphoreType.DMA((2,)),
        ],
        compiler_params=pltpu.CompilerParams(vmem_limit_bytes=16 * 1024 * 1024),
        cost_estimate=pl.CostEstimate(flops=800_000_000, bytes_accessed=6_500_000, transcendentals=0),
        name="update",
    )(*data, near, far, picker, weights)


def device(x, y, z, core):
    return ((y * 4 + z // 2) * 2 * X + x * 2 + core) * 2 + z % 2


X_SHIFT = [[(x * 2 + c, ((x + s) % X) * 2 + c) for x in range(X) for c in range(2)] for s in range(X)]
EVERY = ("cell", "mem", "dp")
PLANES = [[device(x, y, z, 0) for y in range(Y) for z in range(Z)] for x in range(X)]
PLANES += [[device(x, y, z, 1) for x in range(X) for z in range(Z)] for y in range(Y)]
CROSS = [
    [(device(x, y, z, 0), device((x + s) % X, y, z, 0)) for x in range(X) for y in range(Y) for z in range(Z)]
    + [(device(x, y, z, 1), device(x, (y + s) % Y, z, 1)) for x in range(X) for y in range(Y) for z in range(Z)]
    for s in range(X)
]
CORE_SWAP = [(i, i ^ 1) for i in range(2 * X)]


def to_x(piece, s):
    return lax.ppermute(piece, "mem", X_SHIFT[s % X])


def cross(piece, s):
    return lax.ppermute(piece, EVERY, CROSS[s % X])


def after(pieces, others):
    return lax.optimization_barrier((pieces, others))[0]


def swap(piece):
    return lax.ppermute(piece, "mem", CORE_SWAP)


def local(ensemble, data_anom, weighted_innov, profiles, seg_data, seg_profile):
    me_dp, me_mem = lax.axis_index("dp"), lax.axis_index("mem")
    me_x, me_core = me_mem // 2, me_mem % 2
    mem_dev, cells_dev = ensemble.shape
    half_cells = cells_dev // 2
    x_cells = half_cells // X
    own_cells = x_cells // 2

    sent = prepare(data_anom, weighted_innov, seg_data, seg_profile)
    got = lax.all_to_all(sent, EVERY, 0, 0, tiled=True, axis_index_groups=PLANES)

    def state_for(s):
        x_to = (me_x + s) % X
        return lax.dynamic_slice_in_dim(ensemble, me_dp * half_cells + x_to * x_cells, x_cells, 1)

    pieces = [state_for(0)] + [None] * 3
    for s in (2, 1, 3):
        pieces[s] = to_x(state_for(s), s)
    data_rows = 2 * mem_dev
    own = after(got, pieces[1:])[:, :data_rows]
    data_near = [got] + [None] * 3
    for s in (2, 1, 3):
        data_near[s] = cross(own, s)
    data_far = [swap(d) for d in data_near]
    first = me_core == 0
    lists_near, lists_far = got[:, data_rows:], data_far[0][:, data_rows:]

    state = jnp.concatenate(after(pieces, data_near[1]), axis=0)
    near = lax.dynamic_slice_in_dim(state, me_core * own_cells, own_cells, 1)
    far = swap(lax.dynamic_slice_in_dim(state, (1 - me_core) * own_cells, own_cells, 1))

    picker, weights = choose(lists_near, lists_far, profiles, own_cells // 128, data_anom.shape[1])
    new_near, new_far = run_update(data_near + data_far, near, far, picker, weights)

    across = slice(2 * mem_dev, 3 * mem_dev)
    near2 = to_x(new_near[across], 2)
    back_far = swap(new_far)
    far2 = to_x(back_far[across], 2)
    new = jnp.concatenate([jnp.where(first, new_near, back_far), jnp.where(first, back_far, new_near)], axis=1)
    out = jnp.zeros((mem_dev, half_cells), jnp.bfloat16)

    def place(out, piece, s, start):
        return lax.dynamic_update_slice_in_dim(out, piece, ((me_x + s) % X) * x_cells + start, 1)

    out = place(out, new[:mem_dev], 0, 0)
    backs = [to_x(new[s * mem_dev : (s + 1) * mem_dev], -s) for s in (1, 3)]
    out = place(out, near2, 2, me_core * own_cells)
    out = place(out, far2, 2, (1 - me_core) * own_cells)
    out = place(out, backs[0], 1, 0)
    return place(out, backs[1], 3, 0)


def solution(mesh):
    placed = (
        P("mem", "cell"),
        P("mem", ("cell", "dp")),
        P("mem", ("cell", "dp")),
        P(),
        P(("cell", "dp"), None),
        P(("cell", "dp"), None),
    )
    return jax.shard_map(
        local, mesh=mesh, in_specs=placed, out_specs=P("mem", ("cell", "dp")), check_vma=False
    )
```

```python
import jax
import jax.numpy as jnp
from jax import lax
from jax.experimental import pallas as pl
from jax.experimental.pallas import tpu as pltpu
from jax.sharding import PartitionSpec as P

M = 256
EMPTY = 512
X, Y, Z, GROUPS = 4, 4, 8, 32
LIST_ROWS = 8
DN_NT = (((1,), (1,)), ((), ()))
DN_TN = (((0,), (0,)), ((), ()))


def prepare_kernel(anom_hbm, innov_hbm, seg_hbm, prof_hbm, sent_ref, data, lists, sems):
    sources = (anom_hbm, innov_hbm, seg_hbm, prof_hbm)
    targets = (data.at[0], data.at[1], lists.at[0], lists.at[1])
    loads = [pltpu.make_async_copy(src, dst, sems.at[i]) for i, (src, dst) in enumerate(zip(sources, targets))]
    for load in loads:
        load.start()
    me_cell, me_dp, me_mem = (lax.axis_index(n) for n in ("cell", "dp", "mem"))
    _, mem_dev, data_dev = data.shape
    per_group = lists.shape[1]
    per_block = 2 * per_group
    own_blocks = 128 // per_block

    lane_in = lax.broadcasted_iota(jnp.int32, (128, 256), 0)
    lane_out = lax.broadcasted_iota(jnp.int32, (128, 256), 1)
    start = lax.div(me_mem, 2) * 2 * own_blocks + lax.div(lane_out, 128) * own_blocks
    select = jnp.where(lane_in == start + lax.rem(lane_out, own_blocks), 1.0, 0.0).astype(jnp.bfloat16)
    for load in loads[2:]:
        load.wait()
    ids = lists[0]
    ids = jnp.where(ids >= 0, ids - (me_cell * 2 + me_dp) * data_dev, EMPTY)
    both = jnp.concatenate([ids, lists[1]], axis=0).astype(jnp.float32)
    tiles = [both[:, g * 128 : (g + 1) * 128] for g in range(GROUPS)]
    spread = jnp.dot(jnp.concatenate(tiles, axis=0).astype(jnp.bfloat16), select, preferred_element_type=jnp.float32)
    shape = (GROUPS, per_block, 256)
    lane_out = lax.rem(lax.broadcasted_iota(jnp.int32, shape, 2), 128)
    kept = lax.broadcasted_iota(jnp.int32, shape, 1) == lax.div(lane_out, own_blocks)
    packed = jnp.sum(jnp.where(kept, spread.reshape(shape), 0.0), axis=1)
    for load in loads[:2]:
        load.wait()
    block = jnp.concatenate([data[0], data[1]], axis=0)
    filler = jnp.zeros((LIST_ROWS - 2, 128), jnp.float32)
    for g in range(GROUPS):
        rows = jnp.concatenate([packed[g : g + 1, :128], packed[g : g + 1, 128:], filler], axis=0).astype(jnp.bfloat16)
        sent_ref[g] = jnp.concatenate([block, rows], axis=0)


def prepare(anom, innov, seg, prof):
    mem_dev, data_dev = anom.shape
    return pl.pallas_call(
        prepare_kernel,
        out_shape=jax.ShapeDtypeStruct((GROUPS, 2 * mem_dev + LIST_ROWS, data_dev), jnp.bfloat16),
        in_specs=[pl.BlockSpec(memory_space=pl.ANY)] * 4,
        out_specs=pl.BlockSpec(memory_space=pltpu.VMEM),
        scratch_shapes=[
            pltpu.VMEM((2,) + anom.shape, jnp.bfloat16),
            pltpu.VMEM((2,) + seg.shape, jnp.int32),
            pltpu.SemaphoreType.DMA((4,)),
        ],
        compiler_params=pltpu.CompilerParams(vmem_limit_bytes=60 * 1024 * 1024),
        cost_estimate=pl.CostEstimate(flops=10_000_000, bytes_accessed=400_000, transcendentals=0),
        name="prepare",
    )(anom, innov, seg, prof)


def choose_kernel(lists_near, lists_far, table_ref, picker_ref, weights_ref):
    n_block = weights_ref.shape[0]
    data_dev = picker_ref.shape[2] // 2
    me_y = lax.div(lax.axis_index("cell"), 4)
    me_core = lax.rem(lax.axis_index("mem"), 2)
    y_at = [lax.rem(me_y - i + Y, Y) * Z for i in range(Y)]

    row = lax.broadcasted_iota(jnp.int32, (128, 128), 0)
    lane = lax.broadcasted_iota(jnp.int32, (128, 128), 1)
    order = jnp.where(lane == lax.rem(row, 8) * n_block + lax.div(row, 8), 1.0, 0.0).astype(jnp.bfloat16)
    lists = []
    for i in range(Y):
        here = [part[pl.ds(y_at[i], Z)].astype(jnp.float32) for part in (lists_near, lists_far)]
        here = jnp.where(me_core == 0, here[0], here[1])
        wanted = lax.broadcasted_iota(jnp.int32, here.shape, 1) == me_core
        lists.append(jnp.sum(jnp.where(wanted, here, 0.0), axis=1))
    lists = jnp.concatenate(lists + [jnp.zeros((128 - GROUPS, 128), jnp.float32)], axis=0).astype(jnp.bfloat16)
    lists = lax.dot_general(order, lists, DN_NT, preferred_element_type=jnp.float32)
    later = pltpu.roll(lists, 127, 1)
    is_first = lax.rem(row, 8) < 4
    ids = jnp.where(is_first, lists, pltpu.roll(later, 4, 0) + data_dev)
    prof_ids = jnp.where(is_first, pltpu.roll(lists, 124, 0), later)

    table = table_ref[...]
    prof_lanes = lax.broadcasted_iota(jnp.int32, (128, table.shape[0]), 1).astype(jnp.float32)
    lanes = lax.broadcasted_iota(jnp.int32, (128, picker_ref.shape[2]), 1).astype(jnp.float32)
    for pair in range(GROUPS // 2):
        column = slice(2 * pair, 2 * pair + 1)
        picker_ref[pair] = jnp.where(lanes == ids[:, column], 1.0, 0.0).astype(jnp.bfloat16)
        chooser = jnp.where(prof_lanes == prof_ids[:, column], 1.0, 0.0).astype(jnp.bfloat16)
        weight = jnp.dot(chooser, table, preferred_element_type=jnp.float32)
        weights_ref[:, pair * 8 : (pair + 1) * 8] = weight.reshape(n_block, 8, 128)


def choose(lists_near, lists_far, table, n_block, data_dev):
    whole = pl.BlockSpec(memory_space=pltpu.VMEM)
    n_slot = GROUPS * 4
    return pl.pallas_call(
        choose_kernel,
        out_shape=[
            jax.ShapeDtypeStruct((GROUPS // 2, 8 * n_block, 2 * data_dev), jnp.bfloat16),
            jax.ShapeDtypeStruct((n_block, n_slot, 128), jnp.float32),
        ],
        in_specs=[whole] * 3,
        out_specs=[whole] * 2,
        compiler_params=pltpu.CompilerParams(vmem_limit_bytes=8 * 1024 * 1024),
        cost_estimate=pl.CostEstimate(flops=40_000_000, bytes_accessed=2_300_000, transcendentals=0),
        name="choose",
    )(lists_near, lists_far, table)


def select_columns(data, side, picker_ref, cols):
    mem_dev = data[1].shape[1] // 2
    half = X * mem_dev
    n_block = cols.shape[1]
    me_y = lax.div(lax.axis_index("cell"), 4)
    me_mem = lax.axis_index("mem")
    me_x, me_core = lax.div(me_mem, 2), lax.rem(me_mem, 2)
    x_at = [lax.rem(me_x - i + X, X) * Z for i in range(X)]
    y_at = [lax.rem(me_y - i + Y, Y) * Z for i in range(Y)]

    def select(over_x):
        for pair in range(GROUPS // 2):
            i, q = pair // (Z // 2), pair % (Z // 2)

            def piece(s, g, a):
                rows = slice(a * mem_dev, (a + 1) * mem_dev)
                if over_x:
                    return data[s][y_at[i] + 2 * q + g, rows]
                return data[i][x_at[s] + 2 * q + g, rows]

            values = jnp.concatenate(
                [jnp.concatenate([piece(s, g, a) for a in range(2) for s in range(X)], axis=0) for g in range(2)],
                axis=1,
            )
            picked = lax.dot_general(picker_ref[pair], values, DN_NT, preferred_element_type=jnp.float32)
            picked = picked.reshape(n_block, 8, 2 * half)
            for a in range(2):
                cols[a, :, pair * 8 : (pair + 1) * 8] = picked[:, :, a * half : (a + 1) * half]

    pl.when(me_core == side)(lambda: select(True))
    pl.when(me_core != side)(lambda: select(False))


def near_kernel(*refs):
    select_columns(refs[:X], 0, refs[X], refs[X + 1])


def select_near(data, picker, two_m, n_block):
    whole = pl.BlockSpec(memory_space=pltpu.VMEM)
    return pl.pallas_call(
        near_kernel,
        out_shape=jax.ShapeDtypeStruct((2, n_block, GROUPS * 4, X * two_m // 2), jnp.float32),
        in_specs=[whole] * (X + 1),
        out_specs=whole,
        compiler_params=pltpu.CompilerParams(vmem_limit_bytes=8 * 1024 * 1024),
        cost_estimate=pl.CostEstimate(flops=270_000_000, bytes_accessed=5_300_000, transcendentals=0),
        name="select_near",
    )(*data, picker)


def update_kernel(*refs):
    near_hbm, far_hbm, picker_ref, weights, cols_near = refs[X : X + 5]
    out_near, out_far, state, cols, state_sems = refs[X + 5 :]
    half = near_hbm.shape[0]
    n_block = near_hbm.shape[1] // 128

    state_loads = [pltpu.make_async_copy(src, state.at[i], state_sems.at[i]) for i, src in enumerate((near_hbm, far_hbm))]
    for load in state_loads:
        load.start()
    select_columns(refs[:X], 1, picker_ref, cols)

    for load in state_loads:
        load.wait()
    for b in range(n_block):
        spot = pl.ds(b * 128, 128)
        own = jnp.concatenate([state[0, :, spot], state[1, :, spot]], axis=0)
        anom, innov = (jnp.concatenate([cols_near[a, b], cols[a, b]], axis=1).astype(jnp.bfloat16) for a in range(2))
        inner = jnp.dot(anom, own, preferred_element_type=jnp.float32)
        coef = (weights[b] * inner / (M - 1)).astype(jnp.bfloat16)
        corr = lax.dot_general(innov, coef, DN_TN, preferred_element_type=jnp.float32)
        new = (own.astype(jnp.float32) + corr).astype(jnp.bfloat16)
        out_near[:, spot] = new[:half]
        out_far[:, spot] = new[half:]


def run_update(data, near, far, picker, weights, cols_near):
    half, width = near.shape
    n_block = width // 128
    n_slot = GROUPS * 4
    any_space = pl.BlockSpec(memory_space=pl.ANY)
    whole = pl.BlockSpec(memory_space=pltpu.VMEM)
    return pl.pallas_call(
        update_kernel,
        out_shape=[jax.ShapeDtypeStruct(near.shape, jnp.bfloat16)] * 2,
        in_specs=[whole] * len(data) + [any_space] * 2 + [whole] * 3,
        out_specs=[whole] * 2,
        scratch_shapes=[
            pltpu.VMEM((2,) + near.shape, jnp.bfloat16),
            pltpu.VMEM((2, n_block, n_slot, half), jnp.float32),
            pltpu.SemaphoreType.DMA((2,)),
        ],
        compiler_params=pltpu.CompilerParams(vmem_limit_bytes=16 * 1024 * 1024),
        cost_estimate=pl.CostEstimate(flops=800_000_000, bytes_accessed=6_500_000, transcendentals=0),
        name="update",
    )(*data, near, far, picker, weights, cols_near)


def device(x, y, z, core):
    return ((y * 4 + z // 2) * 2 * X + x * 2 + core) * 2 + z % 2


X_SHIFT = [[(x * 2 + c, ((x + s) % X) * 2 + c) for x in range(X) for c in range(2)] for s in range(X)]
EVERY = ("cell", "mem", "dp")
PLANES = [[device(x, y, z, 0) for y in range(Y) for z in range(Z)] for x in range(X)]
PLANES += [[device(x, y, z, 1) for x in range(X) for z in range(Z)] for y in range(Y)]
CROSS = [
    [(device(x, y, z, 0), device((x + s) % X, y, z, 0)) for x in range(X) for y in range(Y) for z in range(Z)]
    + [(device(x, y, z, 1), device(x, (y + s) % Y, z, 1)) for x in range(X) for y in range(Y) for z in range(Z)]
    for s in range(X)
]
CORE_SWAP = [(i, i ^ 1) for i in range(2 * X)]


def to_x(piece, s):
    return lax.ppermute(piece, "mem", X_SHIFT[s % X])


def cross(piece, s):
    return lax.ppermute(piece, EVERY, CROSS[s % X])


def after(pieces, others):
    return lax.optimization_barrier((pieces, others))[0]


def swap(piece):
    return lax.ppermute(piece, "mem", CORE_SWAP)


def local(ensemble, data_anom, weighted_innov, profiles, seg_data, seg_profile):
    me_dp, me_mem = lax.axis_index("dp"), lax.axis_index("mem")
    me_x, me_core = me_mem // 2, me_mem % 2
    mem_dev, cells_dev = ensemble.shape
    half_cells = cells_dev // 2
    x_cells = half_cells // X
    own_cells = x_cells // 2

    sent = prepare(data_anom, weighted_innov, seg_data, seg_profile)
    got = lax.all_to_all(sent, EVERY, 0, 0, tiled=True, axis_index_groups=PLANES)

    def state_for(s):
        x_to = (me_x + s) % X
        return lax.dynamic_slice_in_dim(ensemble, me_dp * half_cells + x_to * x_cells, x_cells, 1)

    pieces = [state_for(0)] + [None] * 3
    for s in (2, 1, 3):
        pieces[s] = to_x(state_for(s), s)
    data_rows = 2 * mem_dev
    own = after(got, pieces[1:])[:, :data_rows]
    data_near = [got] + [None] * 3
    for s in (2, 1, 3):
        data_near[s] = cross(own, s)
    first = me_core == 0
    far_got = swap(got)
    picker, weights = choose(got[:, data_rows:], far_got[:, data_rows:], profiles, own_cells // 128, data_anom.shape[1])
    data_far = [far_got] + [swap(data_near[1]), swap(data_near[2]), swap(data_near[3])]

    state = jnp.concatenate(after(pieces, data_near[1]), axis=0)
    near = lax.dynamic_slice_in_dim(state, me_core * own_cells, own_cells, 1)
    far = swap(lax.dynamic_slice_in_dim(state, (1 - me_core) * own_cells, own_cells, 1))

    cols_near = select_near(data_near, picker, data_rows, own_cells // 128)
    new_near, new_far = run_update(data_far, near, far, picker, weights, cols_near)

    across = slice(2 * mem_dev, 3 * mem_dev)
    near2 = to_x(new_near[across], 2)
    back_far = swap(new_far)
    far2 = to_x(back_far[across], 2)
    new = jnp.concatenate([jnp.where(first, new_near, back_far), jnp.where(first, back_far, new_near)], axis=1)
    out = jnp.zeros((mem_dev, half_cells), jnp.bfloat16)

    def place(out, piece, s, start):
        return lax.dynamic_update_slice_in_dim(out, piece, ((me_x + s) % X) * x_cells + start, 1)

    out = place(out, new[:mem_dev], 0, 0)
    backs = [to_x(new[s * mem_dev : (s + 1) * mem_dev], -s) for s in (1, 3)]
    out = place(out, near2, 2, me_core * own_cells)
    out = place(out, far2, 2, (1 - me_core) * own_cells)
    out = place(out, backs[0], 1, 0)
    return place(out, backs[1], 3, 0)


def solution(mesh):
    placed = (
        P("mem", "cell"),
        P("mem", ("cell", "dp")),
        P("mem", ("cell", "dp")),
        P(),
        P(("cell", "dp"), None),
        P(("cell", "dp"), None),
    )
    return jax.shard_map(
        local, mesh=mesh, in_specs=placed, out_specs=P("mem", ("cell", "dp")), check_vma=False
    )
```

```python
import jax
import jax.numpy as jnp
from jax import lax
from jax.experimental import pallas as pl
from jax.experimental.pallas import tpu as pltpu
from jax.sharding import PartitionSpec as P

M = 256
EMPTY = 512
X, Y, Z, GROUPS = 4, 4, 8, 32
LIST_ROWS = 8
DN_NT = (((1,), (1,)), ((), ()))
DN_TN = (((0,), (0,)), ((), ()))


def prepare_kernel(anom_hbm, innov_hbm, seg_hbm, prof_hbm, sent_ref, data, lists, sems):
    sources = (anom_hbm, innov_hbm, seg_hbm, prof_hbm)
    targets = (data.at[0], data.at[1], lists.at[0], lists.at[1])
    loads = [pltpu.make_async_copy(src, dst, sems.at[i]) for i, (src, dst) in enumerate(zip(sources, targets))]
    for load in loads:
        load.start()
    me_cell, me_dp, me_mem = (lax.axis_index(n) for n in ("cell", "dp", "mem"))
    _, mem_dev, data_dev = data.shape
    per_group = lists.shape[1]
    per_block = 2 * per_group
    own_blocks = 128 // per_block

    lane_in = lax.broadcasted_iota(jnp.int32, (128, 256), 0)
    lane_out = lax.broadcasted_iota(jnp.int32, (128, 256), 1)
    start = lax.div(me_mem, 2) * 2 * own_blocks + lax.div(lane_out, 128) * own_blocks
    select = jnp.where(lane_in == start + lax.rem(lane_out, own_blocks), 1.0, 0.0).astype(jnp.bfloat16)
    for load in loads[2:]:
        load.wait()
    ids = lists[0]
    ids = jnp.where(ids >= 0, ids - (me_cell * 2 + me_dp) * data_dev, EMPTY)
    both = jnp.concatenate([ids, lists[1]], axis=0).astype(jnp.float32)
    tiles = [both[:, g * 128 : (g + 1) * 128] for g in range(GROUPS)]
    spread = jnp.dot(jnp.concatenate(tiles, axis=0).astype(jnp.bfloat16), select, preferred_element_type=jnp.float32)
    shape = (GROUPS, per_block, 256)
    lane_out = lax.rem(lax.broadcasted_iota(jnp.int32, shape, 2), 128)
    kept = lax.broadcasted_iota(jnp.int32, shape, 1) == lax.div(lane_out, own_blocks)
    packed = jnp.sum(jnp.where(kept, spread.reshape(shape), 0.0), axis=1)
    for load in loads[:2]:
        load.wait()
    block = jnp.concatenate([data[0], data[1]], axis=0)
    filler = jnp.zeros((LIST_ROWS - 2, 128), jnp.float32)
    for g in range(GROUPS):
        rows = jnp.concatenate([packed[g : g + 1, :128], packed[g : g + 1, 128:], filler], axis=0).astype(jnp.bfloat16)
        sent_ref[g] = jnp.concatenate([block, rows], axis=0)


def prepare(anom, innov, seg, prof):
    mem_dev, data_dev = anom.shape
    return pl.pallas_call(
        prepare_kernel,
        out_shape=jax.ShapeDtypeStruct((GROUPS, 2 * mem_dev + LIST_ROWS, data_dev), jnp.bfloat16),
        in_specs=[pl.BlockSpec(memory_space=pl.ANY)] * 4,
        out_specs=pl.BlockSpec(memory_space=pltpu.VMEM),
        scratch_shapes=[
            pltpu.VMEM((2,) + anom.shape, jnp.bfloat16),
            pltpu.VMEM((2,) + seg.shape, jnp.int32),
            pltpu.SemaphoreType.DMA((4,)),
        ],
        compiler_params=pltpu.CompilerParams(vmem_limit_bytes=60 * 1024 * 1024),
        cost_estimate=pl.CostEstimate(flops=10_000_000, bytes_accessed=400_000, transcendentals=0),
        name="prepare",
    )(anom, innov, seg, prof)


def choose_kernel(lists_near, lists_far, table_ref, picker_ref, weights_ref):
    n_block = weights_ref.shape[0]
    data_dev = picker_ref.shape[2] // 2
    me_y = lax.div(lax.axis_index("cell"), 4)
    me_core = lax.rem(lax.axis_index("mem"), 2)
    y_at = [lax.rem(me_y - i + Y, Y) * Z for i in range(Y)]

    row = lax.broadcasted_iota(jnp.int32, (128, 128), 0)
    lane = lax.broadcasted_iota(jnp.int32, (128, 128), 1)
    order = jnp.where(lane == lax.rem(row, 8) * n_block + lax.div(row, 8), 1.0, 0.0).astype(jnp.bfloat16)
    lists = []
    for i in range(Y):
        here = [part[pl.ds(y_at[i], Z)].astype(jnp.float32) for part in (lists_near, lists_far)]
        here = jnp.where(me_core == 0, here[0], here[1])
        wanted = lax.broadcasted_iota(jnp.int32, here.shape, 1) == me_core
        lists.append(jnp.sum(jnp.where(wanted, here, 0.0), axis=1))
    lists = jnp.concatenate(lists + [jnp.zeros((128 - GROUPS, 128), jnp.float32)], axis=0).astype(jnp.bfloat16)
    lists = lax.dot_general(order, lists, DN_NT, preferred_element_type=jnp.float32)
    later = pltpu.roll(lists, 127, 1)
    is_first = lax.rem(row, 8) < 4
    ids = jnp.where(is_first, lists, pltpu.roll(later, 4, 0) + data_dev)
    prof_ids = jnp.where(is_first, pltpu.roll(lists, 124, 0), later)

    table = table_ref[...]
    prof_lanes = lax.broadcasted_iota(jnp.int32, (128, table.shape[0]), 1).astype(jnp.float32)
    lanes = lax.broadcasted_iota(jnp.int32, (128, picker_ref.shape[2]), 1).astype(jnp.float32)
    for pair in range(GROUPS // 2):
        column = slice(2 * pair, 2 * pair + 1)
        picker_ref[pair] = jnp.where(lanes == ids[:, column], 1.0, 0.0).astype(jnp.bfloat16)
        chooser = jnp.where(prof_lanes == prof_ids[:, column], 1.0, 0.0).astype(jnp.bfloat16)
        weight = jnp.dot(chooser, table, preferred_element_type=jnp.float32)
        weights_ref[:, pair * 8 : (pair + 1) * 8] = weight.reshape(n_block, 8, 128)


def choose(lists_near, lists_far, table, n_block, data_dev):
    whole = pl.BlockSpec(memory_space=pltpu.VMEM)
    n_slot = GROUPS * 4
    return pl.pallas_call(
        choose_kernel,
        out_shape=[
            jax.ShapeDtypeStruct((GROUPS // 2, 8 * n_block, 2 * data_dev), jnp.bfloat16),
            jax.ShapeDtypeStruct((n_block, n_slot, 128), jnp.float32),
        ],
        in_specs=[whole] * 3,
        out_specs=[whole] * 2,
        compiler_params=pltpu.CompilerParams(vmem_limit_bytes=8 * 1024 * 1024),
        cost_estimate=pl.CostEstimate(flops=40_000_000, bytes_accessed=2_300_000, transcendentals=0),
        name="choose",
    )(lists_near, lists_far, table)


def select_columns(data, side, picker_ref, cols):
    mem_dev = data[1].shape[1] // 2
    half = X * mem_dev
    n_block = cols.shape[1]
    me_y = lax.div(lax.axis_index("cell"), 4)
    me_mem = lax.axis_index("mem")
    me_x, me_core = lax.div(me_mem, 2), lax.rem(me_mem, 2)
    x_at = [lax.rem(me_x - i + X, X) * Z for i in range(X)]
    y_at = [lax.rem(me_y - i + Y, Y) * Z for i in range(Y)]

    def select(over_x):
        for pair in range(GROUPS // 2):
            i, q = pair // (Z // 2), pair % (Z // 2)

            def piece(s, g, a):
                rows = slice(a * mem_dev, (a + 1) * mem_dev)
                if over_x:
                    return data[s][y_at[i] + 2 * q + g, rows]
                return data[i][x_at[s] + 2 * q + g, rows]

            values = jnp.concatenate(
                [jnp.concatenate([piece(s, g, a) for a in range(2) for s in range(X)], axis=0) for g in range(2)],
                axis=1,
            )
            picked = lax.dot_general(picker_ref[pair], values, DN_NT, preferred_element_type=jnp.float32)
            picked = picked.reshape(n_block, 8, 2 * half)
            for a in range(2):
                cols[a, :, pair * 8 : (pair + 1) * 8] = picked[:, :, a * half : (a + 1) * half]

    pl.when(me_core == side)(lambda: select(True))
    pl.when(me_core != side)(lambda: select(False))


def near_kernel(*refs):
    select_columns(refs[:X], 0, refs[X], refs[X + 1])


def select_near(data, picker, two_m, n_block):
    whole = pl.BlockSpec(memory_space=pltpu.VMEM)
    return pl.pallas_call(
        near_kernel,
        out_shape=jax.ShapeDtypeStruct((2, n_block, GROUPS * 4, X * two_m // 2), jnp.float32),
        in_specs=[whole] * (X + 1),
        out_specs=whole,
        compiler_params=pltpu.CompilerParams(vmem_limit_bytes=8 * 1024 * 1024),
        cost_estimate=pl.CostEstimate(flops=270_000_000, bytes_accessed=5_300_000, transcendentals=0),
        name="select_near",
    )(*data, picker)


def update_kernel(*refs):
    near_hbm, far_hbm, picker_ref, weights, cols_near = refs[X : X + 5]
    out_near, out_far, state, cols, state_sems = refs[X + 5 :]
    half = near_hbm.shape[0]
    n_block = near_hbm.shape[1] // 128

    state_loads = [pltpu.make_async_copy(src, state.at[i], state_sems.at[i]) for i, src in enumerate((near_hbm, far_hbm))]
    for load in state_loads:
        load.start()
    select_columns(refs[:X], 1, picker_ref, cols)

    for load in state_loads:
        load.wait()
    for b in range(n_block):
        spot = pl.ds(b * 128, 128)
        own = jnp.concatenate([state[0, :, spot], state[1, :, spot]], axis=0)
        anom, innov = (jnp.concatenate([cols_near[a, b], cols[a, b]], axis=1).astype(jnp.bfloat16) for a in range(2))
        inner = jnp.dot(anom, own, preferred_element_type=jnp.float32)
        coef = (weights[b] * inner / (M - 1)).astype(jnp.bfloat16)
        corr = lax.dot_general(innov, coef, DN_TN, preferred_element_type=jnp.float32)
        new = (own.astype(jnp.float32) + corr).astype(jnp.bfloat16)
        out_near[:, spot] = new[:half]
        out_far[:, spot] = new[half:]


def run_update(data, near, far, picker, weights, cols_near):
    half, width = near.shape
    n_block = width // 128
    n_slot = GROUPS * 4
    any_space = pl.BlockSpec(memory_space=pl.ANY)
    whole = pl.BlockSpec(memory_space=pltpu.VMEM)
    return pl.pallas_call(
        update_kernel,
        out_shape=[jax.ShapeDtypeStruct(near.shape, jnp.bfloat16)] * 2,
        in_specs=[whole] * len(data) + [any_space] * 2 + [whole] * 3,
        out_specs=[whole] * 2,
        scratch_shapes=[
            pltpu.VMEM((2,) + near.shape, jnp.bfloat16),
            pltpu.VMEM((2, n_block, n_slot, half), jnp.float32),
            pltpu.SemaphoreType.DMA((2,)),
        ],
        compiler_params=pltpu.CompilerParams(vmem_limit_bytes=16 * 1024 * 1024),
        cost_estimate=pl.CostEstimate(flops=800_000_000, bytes_accessed=6_500_000, transcendentals=0),
        name="update",
    )(*data, near, far, picker, weights, cols_near)


def device(x, y, z, core):
    return ((y * 4 + z // 2) * 2 * X + x * 2 + core) * 2 + z % 2


X_SHIFT = [[(x * 2 + c, ((x + s) % X) * 2 + c) for x in range(X) for c in range(2)] for s in range(X)]
EVERY = ("cell", "mem", "dp")
PLANES = [[device(x, y, z, 0) for y in range(Y) for z in range(Z)] for x in range(X)]
PLANES += [[device(x, y, z, 1) for x in range(X) for z in range(Z)] for y in range(Y)]
CROSS = [
    [(device(x, y, z, 0), device((x + s) % X, y, z, 0)) for x in range(X) for y in range(Y) for z in range(Z)]
    + [(device(x, y, z, 1), device(x, (y + s) % Y, z, 1)) for x in range(X) for y in range(Y) for z in range(Z)]
    for s in range(X)
]
CORE_SWAP = [(i, i ^ 1) for i in range(2 * X)]


def to_x(piece, s):
    return lax.ppermute(piece, "mem", X_SHIFT[s % X])


def cross(piece, s):
    return lax.ppermute(piece, EVERY, CROSS[s % X])


def after(pieces, others):
    return lax.optimization_barrier((pieces, others))[0]


def swap(piece):
    return lax.ppermute(piece, "mem", CORE_SWAP)


def local(ensemble, data_anom, weighted_innov, profiles, seg_data, seg_profile):
    me_dp, me_mem = lax.axis_index("dp"), lax.axis_index("mem")
    me_x, me_core = me_mem // 2, me_mem % 2
    mem_dev, cells_dev = ensemble.shape
    half_cells = cells_dev // 2
    x_cells = half_cells // X
    own_cells = x_cells // 2

    sent = prepare(data_anom, weighted_innov, seg_data, seg_profile)
    got = lax.all_to_all(sent, EVERY, 0, 0, tiled=True, axis_index_groups=PLANES)

    def state_for(s):
        x_to = (me_x + s) % X
        return lax.dynamic_slice_in_dim(ensemble, me_dp * half_cells + x_to * x_cells, x_cells, 1)

    pieces = [state_for(0)] + [None] * 3
    for s in (2, 1, 3):
        pieces[s] = to_x(state_for(s), s)
    data_rows = 2 * mem_dev
    own = after(got, pieces[1:])[:, :data_rows]
    data_near = [got] + [None] * 3
    for s in (2, 1, 3):
        data_near[s] = cross(own, s)
    first = me_core == 0
    far_got = swap(got)
    picker, weights = choose(got[:, data_rows:], far_got[:, data_rows:], profiles, own_cells // 128, data_anom.shape[1])
    data_far = [far_got] + [swap(data_near[1]), swap(data_near[2]), swap(data_near[3])]

    state = jnp.concatenate(after(pieces, data_near[1]), axis=0)
    near = lax.dynamic_slice_in_dim(state, me_core * own_cells, own_cells, 1)
    far = swap(lax.dynamic_slice_in_dim(state, (1 - me_core) * own_cells, own_cells, 1))

    cols_near = select_near(data_near, picker, data_rows, own_cells // 128)
    new_near, new_far = run_update(data_far, near, far, picker, weights, cols_near)

    across = slice(2 * mem_dev, 3 * mem_dev)
    near2 = to_x(new_near[across], 2)
    back_far = swap(new_far)
    far2 = to_x(back_far[across], 2)
    new = jnp.concatenate([jnp.where(first, new_near, back_far), jnp.where(first, back_far, new_near)], axis=1)
    out = jnp.zeros((mem_dev, half_cells), jnp.bfloat16)

    def place(out, piece, s, start):
        return lax.dynamic_update_slice_in_dim(out, piece, ((me_x + s) % X) * x_cells + start, 1)

    out = place(out, new[:mem_dev], 0, 0)
    backs = [to_x(new[s * mem_dev : (s + 1) * mem_dev], -s) for s in (1, 3)]
    out = place(out, near2, 2, me_core * own_cells)
    out = place(out, backs[0], 1, 0)
    out = place(out, backs[1], 3, 0)
    return place(out, far2, 2, (1 - me_core) * own_cells)


def solution(mesh):
    placed = (
        P("mem", "cell"),
        P("mem", ("cell", "dp")),
        P("mem", ("cell", "dp")),
        P(),
        P(("cell", "dp"), None),
        P(("cell", "dp"), None),
    )
    return jax.shard_map(
        local, mesh=mesh, in_specs=placed, out_specs=P("mem", ("cell", "dp")), check_vma=False
    )
```
